32 devices in a mesh: az: 8 (over z, y), ax: 4 (over x, core).
Axes of the slice: x: 2, y: 2, z: 4, core: 2. Of those that a mesh axis runs over, the one named last changes fastest.
Arguments:
- start_field: float32 [16, 3, 16, 32, 512], P(None, None, 'az', 'ax'), may hold values from -4 to 4
- reluctivity: float32 [3, 16, 32, 512], P(None, 'az', 'ax'), may hold values from 0.05 to 1
- lamination: int32 [16, 32, 512], P('az', 'ax'), may hold values 0 or 1
- magnets: int32 [16, 32, 512], P('az', 'ax'), may hold values 0 or 1
- region_ids: int32 [16, 32, 512], P('az', 'ax'), may hold values from 0 to 31, as said below
- pieces: float32 [3, 16, 32], P(None, None, 'az'), may hold values from -5 to 5
- slot_map: int32 [16, 32], replicated, may hold values from 0 to 31, each once within a row
Outputs:
- solution_field: float32 [16, 3, 16, 32, 512], P(None, None, 'az', 'ax')
- residual: float32 [16, 3, 16, 32, 512], P(None, None, 'az', 'ax')
The draws below stay inside these ranges and needn't reach their ends.
Inputs may be any that keep to these rules, and one draw needn't show every extreme that they name: `region_ids`: a cell of azimuthal sector s, the cells s * 2 to (s + 1) * 2 - 1 along the azimuth, holds a slot from s * 4 to (s + 1) * 4 - 1. `slot_map`: each row is a permutation.
All inputs are finite; a program needn't handle non-finite values. No bound on the sum of `lamination` or of `magnets` on one device may be relied on, other than what follows from the above.
Results may differ from the reference program's by a relative error of at most 0.00002.
Values sent between devices are 32-bit elements; how exact they have to be, the bound alone decides.
A program may use at most 128 MiB of HBM per device.

```python
import math
import jax
import jax.numpy as jnp
from jax import lax

DEVS = 16
REG_DEV = 4
CA = 2
R = 512
NA = 16
NZ = 32
REGIONS = 32


def draw_region_ids(key, part):
    local = jax.random.randint(key, (NA, NZ, R), 0, REG_DEV)
    sector = (jnp.arange(NA) // CA).astype(jnp.int32)
    return (sector[:, None, None] * REG_DEV + local).astype(jnp.int32)


def touch_ends(values, rng, least, largest):
    longest = values.shape.index(max(values.shape))
    spots = []
    for shift in (0, 1):
        where = [jax.random.randint(jax.random.fold_in(rng, axis), (), 0, length) for axis, length in enumerate(values.shape)]
        where[longest] = (where[longest] + shift) % values.shape[longest]
        spots.append(tuple(where))
    return values.at[spots[0]].set(least).at[spots[1]].set(largest)


def levels(rng, dims, shards, low, largest):
    level = 1.0
    for dim, parts in shards:
        draws = jax.random.uniform(jax.random.fold_in(jax.random.fold_in(rng, 6), dim), (parts,), jnp.float32, low / len(shards), largest / len(shards))
        level = level * jnp.repeat(jnp.exp(draws), dims[dim] // parts).reshape((-1,) + (1,) * (len(dims) - 1 - dim))
    return level


def bell_draw(stream_key, extent, spread, reach, shards=(), kind=jnp.bfloat16):
    values = spread * jax.random.normal(stream_key, extent, jnp.float32)
    if shards:
        values = values * levels(stream_key, extent, shards, -0.22, 0.18)
    return jnp.clip(values, -reach, reach).astype(kind)


def setup_inputs(seed: int = 0) -> dict:
    keys = jax.random.split(jax.random.key(seed), 8)
    return {
        "start_field": bell_draw(keys[0], (DEVS, 3, NA, NZ, R), 0.5, 4.0, ((2, 8), (3, 4)), jnp.float32),
        "reluctivity": jnp.clip(jnp.exp(math.log(1.0) - 2.9957323 * jax.random.uniform(keys[1], (3, NA, NZ, R), jnp.float32) ** levels(keys[1], (3, NA, NZ, R), ((1, 8), (2, 4)), -0.2, 0.2)), 0.05, 1.0),
        "lamination": touch_ends((jax.random.randint(keys[2], (NA, NZ, R), 0, 2) < 1).astype(jnp.int32), jax.random.fold_in(keys[2], 1), 0, 1),
        "magnets": touch_ends((jax.random.randint(keys[3], (NA, NZ, R), 0, 3) < 1).astype(jnp.int32), jax.random.fold_in(keys[3], 1), 0, 1),
        "region_ids": draw_region_ids(jax.random.fold_in(keys[7], 71), 0),
        "pieces": bell_draw(keys[5], (3, DEVS, REGIONS), 1.0, 5.0, ((2, 8),), jnp.float32),
        "slot_map": jax.vmap(lambda own: jax.random.permutation(own, REGIONS))(jax.random.split(keys[6], DEVS)).reshape((DEVS, REGIONS)).astype(jnp.int32),
    }


mass_term = 1.0
cheb_centre = 8.5
cheb_halfwidth = 7.5
cheb_sigma = cheb_centre / cheb_halfwidth
rho_first = 1.0 / cheb_sigma
rho_second = 1.0 / (2.0 * cheb_sigma - rho_first)


def forward_az(values):
    return jnp.roll(values, -1, axis=0) - values


def forward_ax(values):
    return jnp.concatenate([values[:, 1:], jnp.zeros_like(values[:, :1])], axis=1) - values


def forward_radial(values):
    return jnp.concatenate([values[..., 1:], jnp.zeros_like(values[..., :1])], axis=-1) - values


def backward_az(values):
    return values - jnp.roll(values, 1, axis=0)


def backward_ax(values):
    return values - jnp.concatenate([jnp.zeros_like(values[:, :1]), values[:, :-1]], axis=1)


def backward_radial(values):
    return values - jnp.concatenate([jnp.zeros_like(values[..., :1]), values[..., :-1]], axis=-1)


def residual_of(field, reluct, source):
    flux = jnp.stack([
        forward_ax(field[2]) - forward_radial(field[1]),
        forward_radial(field[0]) - forward_az(field[2]),
        forward_az(field[1]) - forward_ax(field[0])], axis=0)
    intensity = reluct * (flux - source)
    curl = jnp.stack([
        backward_ax(intensity[2]) - backward_radial(intensity[1]),
        backward_radial(intensity[0]) - backward_az(intensity[2]),
        backward_az(intensity[1]) - backward_ax(intensity[0])], axis=0)
    return -curl - mass_term * field


def reference(start_field, reluctivity, lamination, magnets, region_ids, pieces, slot_map):
    axial = jnp.array([0.0, 1.0, 0.0], jnp.float32)
    reluct = reluctivity * (1.0 + 3.0 * lamination.astype(jnp.float32)[None] * axial[:, None, None, None])
    magnet_float = magnets.astype(jnp.float32)

    def one_deviation(index):
        table = pieces[:, index]
        slots = slot_map[index][region_ids]
        source = jnp.take(table, slots, axis=1) * magnet_float[None]
        start = start_field[index]
        first_res = residual_of(start, reluct, source)
        first_dir = first_res / cheb_centre
        middle = start + first_dir
        second_res = residual_of(middle, reluct, source)
        second_dir = (rho_second * rho_first) * first_dir + (2.0 * rho_second / cheb_halfwidth) * second_res
        final = middle + second_dir
        return final, residual_of(final, reluct, source)

    solution_field, residual = lax.map(one_deviation, jnp.arange(DEVS, dtype=jnp.int32))
    return (solution_field, residual)
```

```python
import functools

import jax
import jax.numpy as jnp
from jax import lax
from jax.experimental import pallas as pl
from jax.experimental.pallas import tpu as pltpu
from jax.sharding import PartitionSpec as P

mass_term = 1.0
cheb_centre = 8.5
cheb_halfwidth = 7.5
cheb_sigma = cheb_centre / cheb_halfwidth
rho_first = 1.0 / cheb_sigma
rho_second = 1.0 / (2.0 * cheb_sigma - rho_first)

MESH = pl.DeviceIdType.MESH
F32 = jnp.float32
LEVELS = 3


def kernel(
    n_az, n_ax, devs, cells, slots,
    start, rel, lam, mag, reg, pcs, smap,
    sol, res,
    X, D0, I, NS, RS, G, PG, TAB, ZA, ZI, AA, AI, SA, SI,
    in_loc, in_s, in_r, g_s, g_r, p_s, p_r,
    za_s, za_r, zi_s, zi_r, aa_s, aa_r, ai_s, ai_r, o_s, o_r, o_l,
):
    half = devs // 2
    planes = 2 * cells
    rows, radial = X.shape[-2], X.shape[-1]
    az, ax = lax.axis_index("az"), lax.axis_index("ax")
    side = lax.rem(az, 2)
    partner = az + 1 - 2 * side
    up, down = lax.rem(az + 2, n_az), lax.rem(az + n_az - 2, n_az)
    mine = pl.ds(cells * side, cells)
    theirs = pl.ds(cells * (1 - side), cells)
    has_below, has_above = ax > 0, ax < n_ax - 1

    def remote(src, dst, s, r, where):
        return pltpu.make_async_remote_copy(
            src_ref=src, dst_ref=dst, send_sem=s, recv_sem=r, device_id=where, device_id_type=MESH
        )

    def local_in():
        return pltpu.make_async_copy(start.at[pl.ds(half * side, half)], X.at[0, :, :, mine], in_loc)

    def swap_in(k):
        return remote(
            start.at[half * (1 - side) + k], X.at[0, k, :, mine], in_s.at[k], in_r.at[k], {"az": partner}
        )

    def swap_g():
        return remote(G.at[:, mine], G.at[:, mine], g_s, g_r, {"az": partner})

    def give_pieces(step):
        return remote(PG.at[az], PG.at[az], p_s.at[step], p_r.at[step], {"az": lax.rem(az + step, n_az)})

    def z_a(level, k):
        return remote(
            X.at[level, k, 1:3, 0], ZA.at[level, k], za_s.at[level, k], za_r.at[level, k], {"az": down}
        )

    def z_i(level, k):
        return remote(
            I.at[level, k, 1:3, planes - 1], ZI.at[level, k], zi_s.at[level, k], zi_r.at[level, k], {"az": up}
        )

    def ax_a(level, k):
        return remote(SA.at[level, k], AA.at[level, k], aa_s.at[level, k], aa_r.at[level, k], {"ax": ax - 1})

    def ax_i(level, k):
        return remote(SI.at[level, k], AI.at[level, k], ai_s.at[level, k], ai_r.at[level, k], {"ax": ax + 1})

    def out_away(which, k):
        src, dst = ((X.at[2, k], sol), (RS.at[k], res))[which]
        return remote(
            src.at[:, theirs], dst.at[half * side + k], o_s.at[which, k], o_r.at[which, k], {"az": partner}
        )

    def out_here(which, k):
        src, dst = ((X.at[2, k], sol), (RS.at[k], res))[which]
        return pltpu.make_async_copy(src.at[:, mine], dst.at[half * side + k], o_l.at[which, k])

    local_in().start()
    barrier = pltpu.get_barrier_semaphore()
    for step in range(1, n_az):
        pl.semaphore_signal(
            barrier, inc=1, device_id={"az": lax.rem(az + step, n_az)}, device_id_type=MESH
        )

    @pl.when(has_below)
    def _():
        pl.semaphore_signal(barrier, inc=1, device_id={"ax": ax - 1}, device_id_type=MESH)

    @pl.when(has_above)
    def _():
        pl.semaphore_signal(barrier, inc=1, device_id={"ax": ax + 1}, device_id_type=MESH)

    for p in range(cells):
        G[0, cells * side + p] = rel[0, p]
        G[1, cells * side + p] = rel[1, p] * (1.0 + 3.0 * lam[p].astype(F32))
        G[2, cells * side + p] = rel[2, p]
        G[3, cells * side + p] = jnp.where(mag[p] == 1, reg[p] - az * slots, -1).astype(F32)
    PG[az] = pcs[...]

    pl.semaphore_wait(barrier, n_az - 1 + has_below.astype(jnp.int32) + has_above.astype(jnp.int32))

    swap_in(0).start()
    for step in range(1, n_az):
        give_pieces(step).start()
    swap_g().start()

    def start_in(k, carry):
        swap_in(k).start()
        return carry

    lax.fori_loop(1, half, start_in, 0)

    @pl.when(jnp.logical_not(has_above))
    def _():
        AA[...] = jnp.zeros_like(AA)

    @pl.when(jnp.logical_not(has_below))
    def _():
        AI[...] = jnp.zeros_like(AI)

    row_of = lax.broadcasted_iota(jnp.int32, (rows, radial), 0)
    lane_of = lax.broadcasted_iota(jnp.int32, (rows, radial), 1)

    def next_radial(v):
        return jnp.where(lane_of == radial - 1, 0.0, pltpu.roll(v, radial - 1, 1))

    def prev_radial(v):
        return jnp.where(lane_of == 0, 0.0, pltpu.roll(v, 1, 1))

    def next_axial(v, halo):
        return jnp.where(row_of == rows - 1, halo, pltpu.roll(v, rows - 1, 0))

    def prev_axial(v, halo):
        return jnp.where(row_of == 0, halo, pltpu.roll(v, 1, 0))

    def send_a(level, k):
        z_a(level, k).start()
        for p in range(planes):
            for j, c in enumerate((0, 2)):
                SA[level, k, j * planes + p : j * planes + p + 1, :] = X[level, k, c, p, 0:1, :]

        @pl.when(has_below)
        def _():
            ax_a(level, k).start()

    def sources(k):
        table = TAB[...]
        lane = lax.broadcasted_iota(jnp.int32, table.shape, 1)
        for c in range(3):
            column = jnp.sum(
                jnp.where(lane == c * devs + half * side + k, table, 0.0), axis=1, keepdims=True
            )
            values = [jnp.broadcast_to(column[j : j + 1], (rows, radial)) for j in range(2 * slots)]
            for p in range(planes):
                code = G[3, p]
                total = jnp.zeros((rows, radial), F32)
                for j in range(slots):
                    total = jnp.where(code == float(j), values[p // cells * slots + j], total)
                NS[k, c, p] = G[c, p] * total

    def intensity(level, k):
        z_a(level, k).wait_recv()

        @pl.when(has_above)
        def _():
            ax_a(level, k).wait_recv()

        for p in reversed(range(planes)):
            a0, a1, a2 = X[level, k, 0, p], X[level, k, 1, p], X[level, k, 2, p]
            if p < planes - 1:
                b1, b2 = X[level, k, 1, p + 1], X[level, k, 2, p + 1]
            else:
                b1, b2 = ZA[level, k, 0], ZA[level, k, 1]
            h0 = AA[level, k, p : p + 1, :]
            h2 = AA[level, k, planes + p : planes + p + 1, :]
            f0 = (next_axial(a2, h2) - a2) - (next_radial(a1) - a1)
            f1 = (next_radial(a0) - a0) - (b2 - a2)
            f2 = (b1 - a1) - (next_axial(a0, h0) - a0)
            for c, f in enumerate((f0, f1, f2)):
                value = G[c, p] * f - NS[k, c, p]
                I[level, k, c, p] = value
                if c != 1:
                    at = (0 if c == 0 else planes) + p
                    SI[level, k, at : at + 1, :] = value[rows - 1 : rows, :]
            if p == planes - 1:
                z_i(level, k).start()

        @pl.when(has_above)
        def _():
            ax_i(level, k).start()

    def curl(level, k):
        z_i(level, k).wait_recv()

        @pl.when(has_below)
        def _():
            ax_i(level, k).wait_recv()

        for p in range(planes):
            i0, i1, i2 = I[level, k, 0, p], I[level, k, 1, p], I[level, k, 2, p]
            if p > 0:
                b1, b2 = I[level, k, 1, p - 1], I[level, k, 2, p - 1]
            else:
                b1, b2 = ZI[level, k, 0], ZI[level, k, 1]
            h0 = AI[level, k, p : p + 1, :]
            h2 = AI[level, k, planes + p : planes + p + 1, :]
            c0 = (i2 - prev_axial(i2, h2)) - (i1 - prev_radial(i1))
            c1 = (i0 - prev_radial(i0)) - (i2 - b2)
            c2 = (i1 - b1) - (i0 - prev_axial(i0, h0))
            for c, value in enumerate((c0, c1, c2)):
                field = X[level, k, c, p]
                r = -value - mass_term * field
                if level == 0:
                    d = r * (1.0 / cheb_centre)
                    D0[k, c, p] = d
                    X[1, k, c, p] = field + d
                elif level == 1:
                    d = (rho_second * rho_first) * D0[k, c, p] + (2.0 * rho_second / cheb_halfwidth) * r
                    X[2, k, c, p] = field + d
                else:
                    RS[k, c, p] = r
        if level < 2:
            send_a(level + 1, k)
        if level > 0:
            out_away(level - 1, k).start()
            out_here(level - 1, k).start()

    def stage(s, k):
        if s == 0:
            @pl.when(k == 0)
            def _():
                local_in().wait()

            swap_in(k).wait_recv()
            send_a(0, k)
        elif s == 1:
            @pl.when(k == 0)
            def _():
                for step in range(1, n_az):
                    give_pieces(step).wait_recv()
                own = smap[...]

                def add(p, total):
                    for q in range(slots):
                        total = total + jnp.where(own == p * slots + q, PG[p, q : q + 1, :], 0.0)
                    return total

                TAB[...] = lax.fori_loop(0, n_az, add, jnp.zeros(TAB.shape, F32))
                swap_g().wait_recv()

            sources(k)
            intensity(0, k)
        elif s % 2 == 0:
            curl(s // 2 - 1, k)
        else:
            intensity(s // 2, k)

    stages = 1 + 2 * LEVELS

    def wave(t, carry):
        for s in reversed(range(stages)):
            k = t - s

            @pl.when(jnp.logical_and(k >= 0, k < half))
            def _(s=s, k=k):
                stage(s, k)

        return carry

    lax.fori_loop(0, half + stages - 1, wave, 0)

    for step in range(1, n_az):
        give_pieces(step).wait_send()
    swap_g().wait_send()

    def finish(k, carry):
        swap_in(k).wait_send()
        for level in range(LEVELS):
            z_a(level, k).wait_send()
            z_i(level, k).wait_send()

            @pl.when(has_below)
            def _():
                ax_a(level, k).wait_send()

            @pl.when(has_above)
            def _():
                ax_i(level, k).wait_send()

        for which in range(2):
            out_here(which, k).wait()
            out_away(which, k).wait()
        return carry

    lax.fori_loop(0, half, finish, 0)


def shards(n_az, n_ax, start_field, reluctivity, lamination, magnets, region_ids, pieces, slot_map):
    devs, comps, cells, rows, radial = start_field.shape
    slots = pieces.shape[2]
    half, planes = devs // 2, 2 * cells
    lanes = -(-comps * devs // 128) * 128
    depth = -(-slots // 8) * 8
    wide = jnp.pad(
        jnp.transpose(pieces, (2, 0, 1)).reshape(slots, comps * devs),
        ((0, depth - slots), (0, lanes - comps * devs)),
    )
    base = lax.axis_index("az") // 2 * (2 * slots)
    own = lax.dynamic_slice_in_dim(slot_map, base, 2 * slots, 1).T
    own = jnp.pad(jnp.tile(own, (1, comps)), ((0, 0), (0, lanes - comps * devs)))

    tile = (rows, radial)
    dma = pltpu.SemaphoreType.DMA
    phase = (LEVELS, half)
    vmem, anywhere = pl.BlockSpec(memory_space=pltpu.VMEM), pl.BlockSpec(memory_space=pl.ANY)
    block = (half, comps, planes) + tile
    shape = jax.ShapeDtypeStruct(start_field.shape, F32)
    return pl.pallas_call(
        functools.partial(kernel, n_az, n_ax, devs, cells, slots),
        out_shape=(shape, shape),
        in_specs=[anywhere] + [vmem] * 6,
        out_specs=(anywhere, anywhere),
        scratch_shapes=[
            pltpu.VMEM((LEVELS,) + block, F32),
            pltpu.VMEM(block, F32),
            pltpu.VMEM((LEVELS,) + block, F32),
            pltpu.VMEM(block, F32),
            pltpu.VMEM(block, F32),
            pltpu.VMEM((comps + 1, planes) + tile, F32),
            pltpu.VMEM((n_az, depth, lanes), F32),
            pltpu.VMEM((2 * slots, lanes), F32),
            pltpu.VMEM(phase + (2,) + tile, F32),
            pltpu.VMEM(phase + (2,) + tile, F32),
        ]
        + [pltpu.VMEM(phase + (2 * planes, radial), F32)] * 4
        + [dma, dma((half,)), dma((half,)), dma, dma, dma((n_az,)), dma((n_az,))]
        + [dma(phase)] * 8
        + [dma((2, half))] * 3,
        compiler_params=pltpu.CompilerParams(
            collective_id=0, has_side_effects=True, vmem_limit_bytes=40 * 1024 * 1024
        ),
        cost_estimate=pl.CostEstimate(
            flops=150 * start_field.size, bytes_accessed=12 * start_field.size, transcendentals=0
        ),
    )(start_field, reluctivity, lamination, magnets, region_ids, wide, own)


def solution(mesh):
    placed = (
        P(None, None, "az", "ax", None),
        P(None, "az", "ax", None),
        P("az", "ax", None),
        P("az", "ax", None),
        P("az", "ax", None),
        P(None, None, "az"),
        P(),
    )
    return jax.shard_map(
        functools.partial(shards, mesh.shape["az"], mesh.shape["ax"]),
        mesh=mesh,
        in_specs=placed,
        out_specs=(P(None, None, "az", "ax", None), P(None, None, "az", "ax", None)),
        check_vma=False,
    )
```

```python
import functools

import jax
import jax.numpy as jnp
from jax import lax
from jax.experimental import pallas as pl
from jax.experimental.pallas import tpu as pltpu
from jax.sharding import PartitionSpec as P

mass_term = 1.0
cheb_centre = 8.5
cheb_halfwidth = 7.5
cheb_sigma = cheb_centre / cheb_halfwidth
rho_first = 1.0 / cheb_sigma
rho_second = 1.0 / (2.0 * cheb_sigma - rho_first)

MESH = pl.DeviceIdType.MESH
F32 = jnp.float32
LEVELS = 3


def kernel(
    n_az, n_ax, devs, cells, slots,
    start, rel_in, lam_in, mag_in, reg_in, pcs_in, smap_in,
    sol, res,
    rel, lam, mag, reg, pcs, smap,
    X, D0, I, NS, RS, G, PG, TAB, ZA, ZI, AA, AI, SA, SI,
    ops, in_loc, in_s, in_r, g_s, g_r, p_s, p_r,
    za_s, za_r, zi_s, zi_r, aa_s, aa_r, ai_s, ai_r, o_s, o_r, o_l,
):
    half = devs // 2
    planes = 2 * cells
    rows, radial = X.shape[-2], X.shape[-1]
    az, ax = lax.axis_index("az"), lax.axis_index("ax")
    side = lax.rem(az, 2)
    partner = az + 1 - 2 * side
    up, down = lax.rem(az + 2, n_az), lax.rem(az + n_az - 2, n_az)
    mine = pl.ds(cells * side, cells)
    theirs = pl.ds(cells * (1 - side), cells)
    has_below, has_above = ax > 0, ax < n_ax - 1

    def remote(src, dst, s, r, where):
        return pltpu.make_async_remote_copy(
            src_ref=src, dst_ref=dst, send_sem=s, recv_sem=r, device_id=where, device_id_type=MESH
        )

    def local_in():
        return pltpu.make_async_copy(start.at[pl.ds(half * side, half)], X.at[0, :, :, mine], in_loc)

    def swap_in(k):
        return remote(
            start.at[half * (1 - side) + k], X.at[0, k, :, mine], in_s.at[k], in_r.at[k], {"az": partner}
        )

    def swap_g():
        return remote(G.at[:, mine], G.at[:, mine], g_s, g_r, {"az": partner})

    def give_pieces(step):
        return remote(PG.at[az], PG.at[az], p_s.at[step], p_r.at[step], {"az": lax.rem(az + step, n_az)})

    def z_a(level, k):
        return remote(
            X.at[level, k, 1:3, 0], ZA.at[level, k], za_s.at[level, k], za_r.at[level, k], {"az": down}
        )

    def z_i(level, k):
        return remote(
            I.at[level, k, 1:3, planes - 1], ZI.at[level, k], zi_s.at[level, k], zi_r.at[level, k], {"az": up}
        )

    def ax_a(level, k):
        return remote(SA.at[level, k], AA.at[level, k], aa_s.at[level, k], aa_r.at[level, k], {"ax": ax - 1})

    def ax_i(level, k):
        return remote(SI.at[level, k], AI.at[level, k], ai_s.at[level, k], ai_r.at[level, k], {"ax": ax + 1})

    def out_away(which, k):
        src, dst = ((X.at[2, k], sol), (RS.at[k], res))[which]
        return remote(
            src.at[:, theirs], dst.at[half * side + k], o_s.at[which, k], o_r.at[which, k], {"az": partner}
        )

    def out_here(which, k):
        src, dst = ((X.at[2, k], sol), (RS.at[k], res))[which]
        return pltpu.make_async_copy(src.at[:, mine], dst.at[half * side + k], o_l.at[which, k])

    operands = [
        pltpu.make_async_copy(src, dst, ops.at[j])
        for j, (src, dst) in enumerate(
            ((rel_in, rel), (lam_in, lam), (mag_in, mag), (reg_in, reg), (pcs_in, pcs), (smap_in, smap))
        )
    ]
    for copy in operands:
        copy.start()
    local_in().start()
    barrier = pltpu.get_barrier_semaphore()
    for step in range(1, n_az):
        pl.semaphore_signal(
            barrier, inc=1, device_id={"az": lax.rem(az + step, n_az)}, device_id_type=MESH
        )

    @pl.when(has_below)
    def _():
        pl.semaphore_signal(barrier, inc=1, device_id={"ax": ax - 1}, device_id_type=MESH)

    @pl.when(has_above)
    def _():
        pl.semaphore_signal(barrier, inc=1, device_id={"ax": ax + 1}, device_id_type=MESH)

    for copy in operands:
        copy.wait()
    for p in range(cells):
        G[0, cells * side + p] = rel[0, p]
        G[1, cells * side + p] = rel[1, p] * (1.0 + 3.0 * lam[p].astype(F32))
        G[2, cells * side + p] = rel[2, p]
        G[3, cells * side + p] = jnp.where(mag[p] == 1, reg[p] - az * slots, -1).astype(F32)
    PG[az] = pcs[...]

    pl.semaphore_wait(barrier, n_az - 1 + has_below.astype(jnp.int32) + has_above.astype(jnp.int32))

    swap_in(0).start()
    for step in range(1, n_az):
        give_pieces(step).start()
    swap_g().start()

    def start_in(k, carry):
        swap_in(k).start()
        return carry

    lax.fori_loop(1, half, start_in, 0)

    @pl.when(jnp.logical_not(has_above))
    def _():
        AA[...] = jnp.zeros_like(AA)

    @pl.when(jnp.logical_not(has_below))
    def _():
        AI[...] = jnp.zeros_like(AI)

    row_of = lax.broadcasted_iota(jnp.int32, (rows, radial), 0)
    lane_of = lax.broadcasted_iota(jnp.int32, (rows, radial), 1)

    def next_radial(v):
        return jnp.where(lane_of == radial - 1, 0.0, pltpu.roll(v, radial - 1, 1))

    def prev_radial(v):
        return jnp.where(lane_of == 0, 0.0, pltpu.roll(v, 1, 1))

    def next_axial(v, halo):
        return jnp.where(row_of == rows - 1, halo, pltpu.roll(v, rows - 1, 0))

    def prev_axial(v, halo):
        return jnp.where(row_of == 0, halo, pltpu.roll(v, 1, 0))

    def send_a(level, k):
        z_a(level, k).start()
        for p in range(planes):
            for j, c in enumerate((0, 2)):
                SA[level, k, j * planes + p : j * planes + p + 1, :] = X[level, k, c, p, 0:1, :]

        @pl.when(has_below)
        def _():
            ax_a(level, k).start()

    def sources(k):
        table = TAB[...]
        lane = lax.broadcasted_iota(jnp.int32, table.shape[1:], 1)
        for c in range(3):
            column = jnp.sum(jnp.where(lane == half * side + k, table[c], 0.0), axis=1, keepdims=True)
            values = [jnp.broadcast_to(column[j : j + 1], (rows, radial)) for j in range(2 * slots)]
            for p in range(planes):
                code = G[3, p]
                total = jnp.zeros((rows, radial), F32)
                for j in range(slots):
                    total = jnp.where(code == float(j), values[p // cells * slots + j], total)
                NS[k, c, p] = G[c, p] * total

    def intensity(level, k):
        z_a(level, k).wait_recv()

        @pl.when(has_above)
        def _():
            ax_a(level, k).wait_recv()

        for p in reversed(range(planes)):
            a0, a1, a2 = X[level, k, 0, p], X[level, k, 1, p], X[level, k, 2, p]
            if p < planes - 1:
                b1, b2 = X[level, k, 1, p + 1], X[level, k, 2, p + 1]
            else:
                b1, b2 = ZA[level, k, 0], ZA[level, k, 1]
            h0 = AA[level, k, p : p + 1, :]
            h2 = AA[level, k, planes + p : planes + p + 1, :]
            f0 = (next_axial(a2, h2) - a2) - (next_radial(a1) - a1)
            f1 = (next_radial(a0) - a0) - (b2 - a2)
            f2 = (b1 - a1) - (next_axial(a0, h0) - a0)
            for c, f in enumerate((f0, f1, f2)):
                value = G[c, p] * f - NS[k, c, p]
                I[level, k, c, p] = value
                if c != 1:
                    at = (0 if c == 0 else planes) + p
                    SI[level, k, at : at + 1, :] = value[rows - 1 : rows, :]
            if p == planes - 1:
                z_i(level, k).start()

        @pl.when(has_above)
        def _():
            ax_i(level, k).start()

    def curl(level, k):
        z_i(level, k).wait_recv()

        @pl.when(has_below)
        def _():
            ax_i(level, k).wait_recv()

        for p in range(planes):
            i0, i1, i2 = I[level, k, 0, p], I[level, k, 1, p], I[level, k, 2, p]
            if p > 0:
                b1, b2 = I[level, k, 1, p - 1], I[level, k, 2, p - 1]
            else:
                b1, b2 = ZI[level, k, 0], ZI[level, k, 1]
            h0 = AI[level, k, p : p + 1, :]
            h2 = AI[level, k, planes + p : planes + p + 1, :]
            c0 = (i2 - prev_axial(i2, h2)) - (i1 - prev_radial(i1))
            c1 = (i0 - prev_radial(i0)) - (i2 - b2)
            c2 = (i1 - b1) - (i0 - prev_axial(i0, h0))
            for c, value in enumerate((c0, c1, c2)):
                field = X[level, k, c, p]
                r = -value - mass_term * field
                if level == 0:
                    d = r * (1.0 / cheb_centre)
                    D0[k, c, p] = d
                    X[1, k, c, p] = field + d
                elif level == 1:
                    d = (rho_second * rho_first) * D0[k, c, p] + (2.0 * rho_second / cheb_halfwidth) * r
                    X[2, k, c, p] = field + d
                else:
                    RS[k, c, p] = r
        if level < 2:
            send_a(level + 1, k)
        if level > 0:
            out_away(level - 1, k).start()
            out_here(level - 1, k).start()

    def stage(s, k):
        if s == 0:
            @pl.when(k == 0)
            def _():
                local_in().wait()

            swap_in(k).wait_recv()
            send_a(0, k)
        elif s == 1:
            @pl.when(k == 0)
            def _():
                for step in range(1, n_az):
                    give_pieces(step).wait_recv()
                own = smap[...]

                for c in range(3):
                    def add(p, total, c=c):
                        for q in range(slots):
                            total = total + jnp.where(own == p * slots + q, PG[p, c, q : q + 1, :], 0.0)
                        return total

                    TAB[c] = lax.fori_loop(0, n_az, add, jnp.zeros(own.shape, F32))
                swap_g().wait_recv()

            sources(k)
            intensity(0, k)
        elif s % 2 == 0:
            curl(s // 2 - 1, k)
        else:
            intensity(s // 2, k)

    stages = 1 + 2 * LEVELS

    def wave(t, carry):
        for s in reversed(range(stages)):
            k = t - s

            @pl.when(jnp.logical_and(k >= 0, k < half))
            def _(s=s, k=k):
                stage(s, k)

        return carry

    lax.fori_loop(0, half + stages - 1, wave, 0)

    for step in range(1, n_az):
        give_pieces(step).wait_send()
    swap_g().wait_send()

    def finish(k, carry):
        swap_in(k).wait_send()
        for level in range(LEVELS):
            z_a(level, k).wait_send()
            z_i(level, k).wait_send()

            @pl.when(has_below)
            def _():
                ax_a(level, k).wait_send()

            @pl.when(has_above)
            def _():
                ax_i(level, k).wait_send()

        for which in range(2):
            out_here(which, k).wait()
            out_away(which, k).wait()
        return carry

    lax.fori_loop(0, half, finish, 0)


def shards(n_az, n_ax, start_field, reluctivity, lamination, magnets, region_ids, pieces, slot_map):
    devs, comps, cells, rows, radial = start_field.shape
    slots = pieces.shape[2]
    half, planes = devs // 2, 2 * cells
    by_slot = jnp.transpose(pieces, (0, 2, 1))
    base = lax.axis_index("az") // 2 * (2 * slots)
    own = lax.dynamic_slice_in_dim(slot_map, base, 2 * slots, 1).T

    tile = (rows, radial)
    dma = pltpu.SemaphoreType.DMA
    phase = (LEVELS, half)
    anywhere = pl.BlockSpec(memory_space=pl.ANY)
    block = (half, comps, planes) + tile
    shape = jax.ShapeDtypeStruct(start_field.shape, F32)
    return pl.pallas_call(
        functools.partial(kernel, n_az, n_ax, devs, cells, slots),
        out_shape=(shape, shape),
        in_specs=[anywhere] * 7,
        out_specs=(anywhere, anywhere),
        scratch_shapes=[
            pltpu.VMEM(reluctivity.shape, F32),
            pltpu.VMEM(lamination.shape, jnp.int32),
            pltpu.VMEM(lamination.shape, jnp.int32),
            pltpu.VMEM(lamination.shape, jnp.int32),
            pltpu.VMEM(by_slot.shape, F32),
            pltpu.VMEM(own.shape, jnp.int32),
            pltpu.VMEM((LEVELS,) + block, F32),
            pltpu.VMEM(block, F32),
            pltpu.VMEM((LEVELS,) + block, F32),
            pltpu.VMEM(block, F32),
            pltpu.VMEM(block, F32),
            pltpu.VMEM((comps + 1, planes) + tile, F32),
            pltpu.VMEM((n_az,) + by_slot.shape, F32),
            pltpu.VMEM((comps,) + own.shape, F32),
            pltpu.VMEM(phase + (2,) + tile, F32),
            pltpu.VMEM(phase + (2,) + tile, F32),
        ]
        + [pltpu.VMEM(phase + (2 * planes, radial), F32)] * 4
        + [dma((6,)), dma, dma((half,)), dma((half,)), dma, dma, dma((n_az,)), dma((n_az,))]
        + [dma(phase)] * 8
        + [dma((2, half))] * 3,
        compiler_params=pltpu.CompilerParams(
            collective_id=0, has_side_effects=True, vmem_limit_bytes=60 * 1024 * 1024
        ),
        cost_estimate=pl.CostEstimate(
            flops=150 * start_field.size, bytes_accessed=12 * start_field.size, transcendentals=0
        ),
    )(start_field, reluctivity, lamination, magnets, region_ids, by_slot, own)


def solution(mesh):
    placed = (
        P(None, None, "az", "ax", None),
        P(None, "az", "ax", None),
        P("az", "ax", None),
        P("az", "ax", None),
        P("az", "ax", None),
        P(None, None, "az"),
        P(),
    )
    return jax.shard_map(
        functools.partial(shards, mesh.shape["az"], mesh.shape["ax"]),
        mesh=mesh,
        in_specs=placed,
        out_specs=(P(None, None, "az", "ax", None), P(None, None, "az", "ax", None)),
        check_vma=False,
    )
```

```python
import functools

import jax
import jax.numpy as jnp
from jax import lax
from jax.experimental import pallas as pl
from jax.experimental.pallas import tpu as pltpu
from jax.sharding import PartitionSpec as P

mass_term = 1.0
cheb_centre = 8.5
cheb_halfwidth = 7.5
cheb_sigma = cheb_centre / cheb_halfwidth
rho_first = 1.0 / cheb_sigma
rho_second = 1.0 / (2.0 * cheb_sigma - rho_first)

MESH = pl.DeviceIdType.MESH
F32 = jnp.float32
LEVELS = 3


def kernel(
    n_az, n_ax, devs, cells, slots,
    start, rel_in, lam_in, mag_in, reg_in, pcs_in, smap_in,
    sol, res,
    rel, lam, mag, reg, pcs, smap,
    X, D0, I, NS, RS, G, PG, TAB, ZA, ZI, AA, AI, SA, SI,
    XF, IF, RF, HA, HI, FA, FI, SFA, SFI,
    ops, in_loc, in_s, in_r, g_s, g_r, p_s, p_r,
    za_s, za_r, zi_s, zi_r, aa_s, aa_r, ai_s, ai_r, o_l, f_l,
    xf_s, xf_r, ha_s, ha_r, hi_s, hi_r, fa_s, fa_r, fi_s, fi_r,
):
    half = devs // 2
    planes = 2 * cells
    rows, radial = X.shape[-2], X.shape[-1]
    az, ax = lax.axis_index("az"), lax.axis_index("ax")
    side = lax.rem(az, 2)
    partner = az + 1 - 2 * side
    up, down = lax.rem(az + 2, n_az), lax.rem(az + n_az - 2, n_az)
    mine = pl.ds(cells * side, cells)
    theirs = pl.ds(cells * (1 - side), cells)
    has_below, has_above = ax > 0, ax < n_ax - 1

    def remote(src, dst, s, r, where):
        return pltpu.make_async_remote_copy(
            src_ref=src, dst_ref=dst, send_sem=s, recv_sem=r, device_id=where, device_id_type=MESH
        )

    def local_in():
        return pltpu.make_async_copy(start.at[pl.ds(half * side, half)], X.at[0, :, :, mine], in_loc)

    def swap_in(k):
        return remote(
            start.at[half * (1 - side) + k], X.at[0, k, :, mine], in_s.at[k], in_r.at[k], {"az": partner}
        )

    def swap_g():
        return remote(G.at[:, mine], G.at[:, mine], g_s, g_r, {"az": partner})

    def give_pieces(step):
        return remote(PG.at[az], PG.at[az], p_s.at[step], p_r.at[step], {"az": lax.rem(az + step, n_az)})

    def z_a(level, k):
        return remote(
            X.at[level, k, 1:3, 0], ZA.at[level, k], za_s.at[level, k], za_r.at[level, k], {"az": down}
        )

    def z_i(level, k):
        return remote(
            I.at[level, k, 1:3, planes - 1], ZI.at[level, k], zi_s.at[level, k], zi_r.at[level, k], {"az": up}
        )

    def ax_a(level, k):
        return remote(SA.at[level, k], AA.at[level, k], aa_s.at[level, k], aa_r.at[level, k], {"ax": ax - 1})

    def ax_i(level, k):
        return remote(SI.at[level, k], AI.at[level, k], ai_s.at[level, k], ai_r.at[level, k], {"ax": ax + 1})

    def out_here(which, k):
        src, dst = ((X.at[2, k, :, mine], sol), (RS.at[k], res))[which]
        return pltpu.make_async_copy(src, dst.at[half * side + k], o_l.at[which, k])

    def out_foreign(which, k):
        src, dst = ((XF.at[k], sol), (RF.at[k], res))[which]
        return pltpu.make_async_copy(src, dst.at[half * (1 - side) + k], f_l.at[which, k])

    def hand_x(k):
        return remote(X.at[2, k, :, theirs], XF.at[k], xf_s.at[k], xf_r.at[k], {"az": partner})

    def hand_a(k, src):
        return remote(src, HA.at[k], ha_s.at[k], ha_r.at[k], {"az": partner})

    def hand_i(k, src):
        return remote(src, HI.at[k], hi_s.at[k], hi_r.at[k], {"az": partner})

    def far_a(k):
        return remote(SFA.at[k], FA.at[k], fa_s.at[k], fa_r.at[k], {"ax": ax - 1})

    def far_i(k):
        return remote(SFI.at[k], FI.at[k], fi_s.at[k], fi_r.at[k], {"ax": ax + 1})

    operands = [
        pltpu.make_async_copy(src, dst, ops.at[j])
        for j, (src, dst) in enumerate(
            ((rel_in, rel), (lam_in, lam), (mag_in, mag), (reg_in, reg), (pcs_in, pcs), (smap_in, smap))
        )
    ]
    for copy in operands:
        copy.start()
    local_in().start()
    barrier = pltpu.get_barrier_semaphore()
    for step in range(1, n_az):
        pl.semaphore_signal(
            barrier, inc=1, device_id={"az": lax.rem(az + step, n_az)}, device_id_type=MESH
        )

    @pl.when(has_below)
    def _():
        pl.semaphore_signal(barrier, inc=1, device_id={"ax": ax - 1}, device_id_type=MESH)

    @pl.when(has_above)
    def _():
        pl.semaphore_signal(barrier, inc=1, device_id={"ax": ax + 1}, device_id_type=MESH)

    for copy in operands:
        copy.wait()
    for p in range(cells):
        G[0, cells * side + p] = rel[0, p]
        G[1, cells * side + p] = rel[1, p] * (1.0 + 3.0 * lam[p].astype(F32))
        G[2, cells * side + p] = rel[2, p]
        G[3, cells * side + p] = jnp.where(mag[p] == 1, reg[p] - az * slots, -1).astype(F32)
    PG[az] = pcs[...]

    pl.semaphore_wait(barrier, n_az - 1 + has_below.astype(jnp.int32) + has_above.astype(jnp.int32))

    swap_in(0).start()
    for step in range(1, n_az):
        give_pieces(step).start()
    swap_g().start()

    def start_in(k, carry):
        swap_in(k).start()
        return carry

    lax.fori_loop(1, half, start_in, 0)

    @pl.when(jnp.logical_not(has_above))
    def _():
        AA[...] = jnp.zeros_like(AA)
        FA[...] = jnp.zeros_like(FA)

    @pl.when(jnp.logical_not(has_below))
    def _():
        AI[...] = jnp.zeros_like(AI)
        FI[...] = jnp.zeros_like(FI)

    row_of = lax.broadcasted_iota(jnp.int32, (rows, radial), 0)
    lane_of = lax.broadcasted_iota(jnp.int32, (rows, radial), 1)

    def next_radial(v):
        return jnp.where(lane_of == radial - 1, 0.0, pltpu.roll(v, radial - 1, 1))

    def prev_radial(v):
        return jnp.where(lane_of == 0, 0.0, pltpu.roll(v, 1, 1))

    def next_axial(v, halo):
        return jnp.where(row_of == rows - 1, halo, pltpu.roll(v, rows - 1, 0))

    def prev_axial(v, halo):
        return jnp.where(row_of == 0, halo, pltpu.roll(v, 1, 0))

    def flux_of(a0, a1, a2, b1, b2, h0, h2):
        return (
            (next_axial(a2, h2) - a2) - (next_radial(a1) - a1),
            (next_radial(a0) - a0) - (b2 - a2),
            (b1 - a1) - (next_axial(a0, h0) - a0),
        )

    def curl_of(i0, i1, i2, b1, b2, h0, h2):
        return (
            (i2 - prev_axial(i2, h2)) - (i1 - prev_radial(i1)),
            (i0 - prev_radial(i0)) - (i2 - b2),
            (i1 - b1) - (i0 - prev_axial(i0, h0)),
        )

    def send_a(level, k):
        z_a(level, k).start()
        for p in range(planes):
            for j, c in enumerate((0, 2)):
                SA[level, k, j * planes + p : j * planes + p + 1, :] = X[level, k, c, p, 0:1, :]

        @pl.when(has_below)
        def _():
            ax_a(level, k).start()

    def sources(k):
        table = TAB[...]
        lane = lax.broadcasted_iota(jnp.int32, table.shape[1:], 1)
        for c in range(3):
            column = jnp.sum(jnp.where(lane == half * side + k, table[c], 0.0), axis=1, keepdims=True)
            values = [jnp.broadcast_to(column[j : j + 1], (rows, radial)) for j in range(2 * slots)]
            for p in range(planes):
                code = G[3, p]
                total = jnp.zeros((rows, radial), F32)
                for j in range(slots):
                    total = jnp.where(code == float(j), values[p // cells * slots + j], total)
                NS[k, c, p] = G[c, p] * total

    def intensity(level, k):
        z_a(level, k).wait_recv()

        @pl.when(has_above)
        def _():
            ax_a(level, k).wait_recv()

        for p in reversed(range(planes)):
            a0, a1, a2 = X[level, k, 0, p], X[level, k, 1, p], X[level, k, 2, p]
            if p < planes - 1:
                b1, b2 = X[level, k, 1, p + 1], X[level, k, 2, p + 1]
            else:
                b1, b2 = ZA[level, k, 0], ZA[level, k, 1]
            h0 = AA[level, k, p : p + 1, :]
            h2 = AA[level, k, planes + p : planes + p + 1, :]
            flux = flux_of(a0, a1, a2, b1, b2, h0, h2)
            for c, f in enumerate(flux):
                value = G[c, p] * f - NS[k, c, p]
                I[level, k, c, p] = value
                if c != 1:
                    at = (0 if c == 0 else planes) + p
                    SI[level, k, at : at + 1, :] = value[rows - 1 : rows, :]
            if p == planes - 1:
                z_i(level, k).start()

        @pl.when(has_above)
        def _():
            ax_i(level, k).start()

    def curl(level, k):
        z_i(level, k).wait_recv()

        @pl.when(has_below)
        def _():
            ax_i(level, k).wait_recv()

        for p in range(planes):
            i0, i1, i2 = I[level, k, 0, p], I[level, k, 1, p], I[level, k, 2, p]
            if p > 0:
                b1, b2 = I[level, k, 1, p - 1], I[level, k, 2, p - 1]
            else:
                b1, b2 = ZI[level, k, 0], ZI[level, k, 1]
            h0 = AI[level, k, p : p + 1, :]
            h2 = AI[level, k, planes + p : planes + p + 1, :]
            turned = curl_of(i0, i1, i2, b1, b2, h0, h2)
            for c, value in enumerate(turned):
                field = X[level, k, c, p]
                r = -value - mass_term * field
                if level == 0:
                    d = r * (1.0 / cheb_centre)
                    D0[k, c, p] = d
                    X[1, k, c, p] = field + d
                else:
                    d = (rho_second * rho_first) * D0[k, c, p] + (2.0 * rho_second / cheb_halfwidth) * r
                    X[2, k, c, p] = field + d
        send_a(level + 1, k)
        if level == 1:
            hand_x(k).start()
            out_here(0, k).start()

    def hand_ahead(k):
        @pl.when(side == 0)
        def _():
            hand_a(k, ZA.at[2, k]).start()
            hand_i(k, I.at[2, k, 1:3, cells - 1]).start()

        @pl.when(side == 1)
        def _():
            hand_a(k, X.at[2, k, 1:3, cells]).start()

    def last_curl(k):
        z_i(2, k).wait_recv()

        @pl.when(side == 1)
        def _():
            hand_i(k, ZI.at[2, k]).start()

        @pl.when(has_below)
        def _():
            ax_i(2, k).wait_recv()

        for q in range(cells):
            p = cells * side + q
            i0, i1, i2 = I[2, k, 0, p], I[2, k, 1, p], I[2, k, 2, p]
            if q > 0:
                b1, b2 = I[2, k, 1, p - 1], I[2, k, 2, p - 1]
            else:
                b1 = jnp.where(side == 0, ZI[2, k, 0], I[2, k, 1, cells - 1])
                b2 = jnp.where(side == 0, ZI[2, k, 1], I[2, k, 2, cells - 1])
            h0, h2 = (
                jnp.where(side == 0, AI[2, k, at : at + 1, :], AI[2, k, at + cells : at + cells + 1, :])
                for at in (q, planes + q)
            )
            for c, value in enumerate(curl_of(i0, i1, i2, b1, b2, h0, h2)):
                RS[k, c, q] = -value - mass_term * X[2, k, c, p]
        out_here(1, k).start()

    def far_start(k):
        hand_x(k).wait_recv()
        out_foreign(0, k).start()
        for q in range(cells):
            for j, c in enumerate((0, 2)):
                SFA[k, j * cells + q : j * cells + q + 1, :] = XF[k, c, q, 0:1, :]

        @pl.when(has_below)
        def _():
            far_a(k).start()

    def far_intensity(k):
        hand_a(k, ZA.at[2, k]).wait_recv()

        @pl.when(has_above)
        def _():
            far_a(k).wait_recv()

        table = TAB[...]
        lane = lax.broadcasted_iota(jnp.int32, table.shape[1:], 1)
        for q in range(cells):
            p = cells * side + q
            a0, a1, a2 = XF[k, 0, q], XF[k, 1, q], XF[k, 2, q]
            if q < cells - 1:
                b1, b2 = XF[k, 1, q + 1], XF[k, 2, q + 1]
            else:
                b1, b2 = HA[k, 0], HA[k, 1]
            h0, h2 = FA[k, q : q + 1, :], FA[k, cells + q : cells + q + 1, :]
            code = G[3, p]
            for c, f in enumerate(flux_of(a0, a1, a2, b1, b2, h0, h2)):
                column = jnp.sum(
                    jnp.where(lane == half * (1 - side) + k, table[c], 0.0), axis=1, keepdims=True
                )
                total = jnp.zeros((rows, radial), F32)
                for j in range(slots):
                    own = jnp.where(side == 0, column[j : j + 1], column[slots + j : slots + j + 1])
                    total = jnp.where(code == float(j), jnp.broadcast_to(own, (rows, radial)), total)
                value = G[c, p] * (f - total)
                IF[k, c, q] = value
                if c != 1:
                    at = (0 if c == 0 else cells) + q
                    SFI[k, at : at + 1, :] = value[rows - 1 : rows, :]

        @pl.when(has_above)
        def _():
            far_i(k).start()

    def far_curl(k):
        hand_i(k, ZI.at[2, k]).wait_recv()

        @pl.when(has_below)
        def _():
            far_i(k).wait_recv()

        for q in range(cells):
            i0, i1, i2 = IF[k, 0, q], IF[k, 1, q], IF[k, 2, q]
            if q > 0:
                b1, b2 = IF[k, 1, q - 1], IF[k, 2, q - 1]
            else:
                b1, b2 = HI[k, 0], HI[k, 1]
            h0, h2 = FI[k, q : q + 1, :], FI[k, cells + q : cells + q + 1, :]
            for c, value in enumerate(curl_of(i0, i1, i2, b1, b2, h0, h2)):
                RF[k, c, q] = -value - mass_term * XF[k, c, q]
        out_foreign(1, k).start()

    def stage(s, k):
        if s == 0:
            @pl.when(k == 0)
            def _():
                local_in().wait()

            swap_in(k).wait_recv()
            send_a(0, k)
        elif s == 1:
            @pl.when(k == 0)
            def _():
                for step in range(1, n_az):
                    give_pieces(step).wait_recv()
                own = smap[...]

                for c in range(3):
                    def add(p, total, c=c):
                        for q in range(slots):
                            total = total + jnp.where(own == p * slots + q, PG[p, c, q : q + 1, :], 0.0)
                        return total

                    TAB[c] = lax.fori_loop(0, n_az, add, jnp.zeros(own.shape, F32))
                swap_g().wait_recv()

            sources(k)
            intensity(0, k)
        elif s == 5:
            intensity(2, k)
            hand_ahead(k)
        elif s == 6:
            last_curl(k)
            far_start(k)
        elif s == 7:
            far_intensity(k)
        elif s == 8:
            far_curl(k)
        elif s % 2 == 0:
            curl(s // 2 - 1, k)
        else:
            intensity(s // 2, k)

    stages = 3 + 2 * LEVELS

    def wave(t, carry):
        for s in reversed(range(stages)):
            k = t - s

            @pl.when(jnp.logical_and(k >= 0, k < half))
            def _(s=s, k=k):
                stage(s, k)

        return carry

    lax.fori_loop(0, half + stages - 1, wave, 0)

    for step in range(1, n_az):
        give_pieces(step).wait_send()
    swap_g().wait_send()

    def finish(k, carry):
        swap_in(k).wait_send()
        for level in range(LEVELS):
            z_a(level, k).wait_send()
            z_i(level, k).wait_send()

            @pl.when(has_below)
            def _():
                ax_a(level, k).wait_send()

            @pl.when(has_above)
            def _():
                ax_i(level, k).wait_send()

        hand_x(k).wait_send()
        hand_a(k, ZA.at[2, k]).wait_send()
        hand_i(k, ZI.at[2, k]).wait_send()

        @pl.when(has_below)
        def _():
            far_a(k).wait_send()

        @pl.when(has_above)
        def _():
            far_i(k).wait_send()

        for which in range(2):
            out_here(which, k).wait()
            out_foreign(which, k).wait()
        return carry

    lax.fori_loop(0, half, finish, 0)


def shards(n_az, n_ax, start_field, reluctivity, lamination, magnets, region_ids, pieces, slot_map):
    devs, comps, cells, rows, radial = start_field.shape
    slots = pieces.shape[2]
    half, planes = devs // 2, 2 * cells
    by_slot = jnp.transpose(pieces, (0, 2, 1))
    base = lax.axis_index("az") // 2 * (2 * slots)
    own = lax.dynamic_slice_in_dim(slot_map, base, 2 * slots, 1).T

    tile = (rows, radial)
    dma = pltpu.SemaphoreType.DMA
    phase = (LEVELS, half)
    anywhere = pl.BlockSpec(memory_space=pl.ANY)
    block = (half, comps, planes) + tile
    home = (half, comps, cells) + tile
    shape = jax.ShapeDtypeStruct(start_field.shape, F32)
    return pl.pallas_call(
        functools.partial(kernel, n_az, n_ax, devs, cells, slots),
        out_shape=(shape, shape),
        in_specs=[anywhere] * 7,
        out_specs=(anywhere, anywhere),
        scratch_shapes=[
            pltpu.VMEM(reluctivity.shape, F32),
            pltpu.VMEM(lamination.shape, jnp.int32),
            pltpu.VMEM(lamination.shape, jnp.int32),
            pltpu.VMEM(lamination.shape, jnp.int32),
            pltpu.VMEM(by_slot.shape, F32),
            pltpu.VMEM(own.shape, jnp.int32),
            pltpu.VMEM((LEVELS,) + block, F32),
            pltpu.VMEM(block, F32),
            pltpu.VMEM((LEVELS,) + block, F32),
            pltpu.VMEM(block, F32),
            pltpu.VMEM(home, F32),
            pltpu.VMEM((comps + 1, planes) + tile, F32),
            pltpu.VMEM((n_az,) + by_slot.shape, F32),
            pltpu.VMEM((comps,) + own.shape, F32),
            pltpu.VMEM(phase + (2,) + tile, F32),
            pltpu.VMEM(phase + (2,) + tile, F32),
        ]
        + [pltpu.VMEM(phase + (2 * planes, radial), F32)] * 4
        + [pltpu.VMEM(home, F32)] * 3
        + [pltpu.VMEM((half, 2) + tile, F32)] * 2
        + [pltpu.VMEM((half, 2 * cells, radial), F32)] * 4
        + [dma((6,)), dma, dma((half,)), dma((half,)), dma, dma, dma((n_az,)), dma((n_az,))]
        + [dma(phase)] * 8
        + [dma((2, half))] * 2
        + [dma((half,))] * 10,
        compiler_params=pltpu.CompilerParams(
            collective_id=0, has_side_effects=True, vmem_limit_bytes=60 * 1024 * 1024
        ),
        cost_estimate=pl.CostEstimate(
            flops=150 * start_field.size, bytes_accessed=12 * start_field.size, transcendentals=0
        ),
    )(start_field, reluctivity, lamination, magnets, region_ids, by_slot, own)


def solution(mesh):
    placed = (
        P(None, None, "az", "ax", None),
        P(None, "az", "ax", None),
        P("az", "ax", None),
        P("az", "ax", None),
        P("az", "ax", None),
        P(None, None, "az"),
        P(),
    )
    return jax.shard_map(
        functools.partial(shards, mesh.shape["az"], mesh.shape["ax"]),
        mesh=mesh,
        in_specs=placed,
        out_specs=(P(None, None, "az", "ax", None), P(None, None, "az", "ax", None)),
        check_vma=False,
    )
```

```python
import functools

import jax
import jax.numpy as jnp
from jax import lax
from jax.experimental import pallas as pl
from jax.experimental.pallas import tpu as pltpu
from jax.sharding import PartitionSpec as P

mass_term = 1.0
cheb_centre = 8.5
cheb_halfwidth = 7.5
cheb_sigma = cheb_centre / cheb_halfwidth
rho_first = 1.0 / cheb_sigma
rho_second = 1.0 / (2.0 * cheb_sigma - rho_first)

MESH = pl.DeviceIdType.MESH
F32 = jnp.float32
LEVELS = 3
GROUP = 2


def kernel(
    n_az, n_ax, devs, cells, slots,
    start, rel_in, lam_in, mag_in, reg_in, pcs_in, smap_in,
    sol, res,
    rel, lam, mag, reg, pcs, smap,
    X, D0, I, NS, RS, G, PG, TAB, ZA, ZI, AA, AI, SA, SI,
    ops, in_loc, in_s, in_r, g_s, g_r, p_s, p_r,
    za_s, za_r, zi_s, zi_r, aa_s, aa_r, ai_s, ai_r, o_s, o_r, o_l,
):
    half = devs // 2
    planes = 2 * cells
    rows, radial = X.shape[-2], X.shape[-1]
    az, ax = lax.axis_index("az"), lax.axis_index("ax")
    side = lax.rem(az, 2)
    partner = az + 1 - 2 * side
    up, down = lax.rem(az + 2, n_az), lax.rem(az + n_az - 2, n_az)
    mine = pl.ds(cells * side, cells)
    theirs = pl.ds(cells * (1 - side), cells)
    has_below, has_above = ax > 0, ax < n_ax - 1

    def remote(src, dst, s, r, where):
        return pltpu.make_async_remote_copy(
            src_ref=src, dst_ref=dst, send_sem=s, recv_sem=r, device_id=where, device_id_type=MESH
        )

    def local_in():
        return pltpu.make_async_copy(start.at[pl.ds(half * side, half)], X.at[0, :, :, mine], in_loc)

    def swap_in(k):
        return remote(
            start.at[half * (1 - side) + k], X.at[0, k, :, mine], in_s.at[k], in_r.at[k], {"az": partner}
        )

    def swap_g():
        return remote(G.at[:, mine], G.at[:, mine], g_s, g_r, {"az": partner})

    def give_pieces(step):
        return remote(PG.at[az], PG.at[az], p_s.at[step], p_r.at[step], {"az": lax.rem(az + step, n_az)})

    def z_a(level, k):
        return remote(
            X.at[level, k, 1:3, 0], ZA.at[level, k], za_s.at[level, k], za_r.at[level, k], {"az": down}
        )

    def z_i(level, k):
        return remote(
            I.at[level, k, 1:3, planes - 1], ZI.at[level, k], zi_s.at[level, k], zi_r.at[level, k], {"az": up}
        )

    def ax_a(level, k):
        return remote(SA.at[level, k], AA.at[level, k], aa_s.at[level, k], aa_r.at[level, k], {"ax": ax - 1})

    def ax_i(level, k):
        return remote(SI.at[level, k], AI.at[level, k], ai_s.at[level, k], ai_r.at[level, k], {"ax": ax + 1})

    def out_away(which, k):
        src, dst = ((X.at[2, k], sol), (RS.at[k], res))[which]
        return remote(
            src.at[:, theirs], dst.at[half * side + k], o_s.at[which, k], o_r.at[which, k], {"az": partner}
        )

    def out_here(which, k):
        src, dst = ((X.at[2, k], sol), (RS.at[k], res))[which]
        return pltpu.make_async_copy(src.at[:, mine], dst.at[half * side + k], o_l.at[which, k])

    operands = [
        pltpu.make_async_copy(src, dst, ops.at[j])
        for j, (src, dst) in enumerate(
            ((rel_in, rel), (lam_in, lam), (mag_in, mag), (reg_in, reg), (pcs_in, pcs), (smap_in, smap))
        )
    ]
    for copy in operands:
        copy.start()
    local_in().start()
    barrier = pltpu.get_barrier_semaphore()
    for step in range(1, n_az):
        pl.semaphore_signal(
            barrier, inc=1, device_id={"az": lax.rem(az + step, n_az)}, device_id_type=MESH
        )

    @pl.when(has_below)
    def _():
        pl.semaphore_signal(barrier, inc=1, device_id={"ax": ax - 1}, device_id_type=MESH)

    @pl.when(has_above)
    def _():
        pl.semaphore_signal(barrier, inc=1, device_id={"ax": ax + 1}, device_id_type=MESH)

    for copy in operands:
        copy.wait()
    for p in range(cells):
        G[0, cells * side + p] = rel[0, p]
        G[1, cells * side + p] = rel[1, p] * (1.0 + 3.0 * lam[p].astype(F32))
        G[2, cells * side + p] = rel[2, p]
        G[3, cells * side + p] = jnp.where(mag[p] == 1, reg[p] - az * slots, -1).astype(F32)
    PG[az] = pcs[...]

    pl.semaphore_wait(barrier, n_az - 1 + has_below.astype(jnp.int32) + has_above.astype(jnp.int32))

    swap_in(0).start()
    for step in range(1, n_az):
        give_pieces(step).start()
    swap_g().start()

    def start_in(k, carry):
        swap_in(k).start()
        return carry

    lax.fori_loop(1, half, start_in, 0)

    @pl.when(jnp.logical_not(has_above))
    def _():
        AA[...] = jnp.zeros_like(AA)

    @pl.when(jnp.logical_not(has_below))
    def _():
        AI[...] = jnp.zeros_like(AI)

    row_of = lax.broadcasted_iota(jnp.int32, (rows, radial), 0)
    lane_of = lax.broadcasted_iota(jnp.int32, (rows, radial), 1)

    def next_radial(v):
        return jnp.where(lane_of == radial - 1, 0.0, pltpu.roll(v, radial - 1, 1))

    def prev_radial(v):
        return jnp.where(lane_of == 0, 0.0, pltpu.roll(v, 1, 1))

    def next_axial(v, halo):
        return jnp.where(row_of == rows - 1, halo, pltpu.roll(v, rows - 1, 0))

    def prev_axial(v, halo):
        return jnp.where(row_of == 0, halo, pltpu.roll(v, 1, 0))

    def send_a(level, k):
        z_a(level, k).start()
        for p in range(planes):
            for j, c in enumerate((0, 2)):
                SA[level, k, j * planes + p : j * planes + p + 1, :] = X[level, k, c, p, 0:1, :]

        @pl.when(has_below)
        def _():
            ax_a(level, k).start()

    def sources(k):
        table = TAB[...]
        lane = lax.broadcasted_iota(jnp.int32, table.shape[1:], 1)
        for c in range(3):
            column = jnp.sum(jnp.where(lane == half * side + k, table[c], 0.0), axis=1, keepdims=True)
            values = [jnp.broadcast_to(column[j : j + 1], (rows, radial)) for j in range(2 * slots)]
            for p in range(planes):
                code = G[3, p]
                total = jnp.zeros((rows, radial), F32)
                for j in range(slots):
                    total = jnp.where(code == float(j), values[p // cells * slots + j], total)
                NS[k, c, p] = G[c, p] * total

    def intensity(level, k):
        z_a(level, k).wait_recv()

        @pl.when(has_above)
        def _():
            ax_a(level, k).wait_recv()

        for p in reversed(range(planes)):
            a0, a1, a2 = X[level, k, 0, p], X[level, k, 1, p], X[level, k, 2, p]
            if p < planes - 1:
                b1, b2 = X[level, k, 1, p + 1], X[level, k, 2, p + 1]
            else:
                b1, b2 = ZA[level, k, 0], ZA[level, k, 1]
            h0 = AA[level, k, p : p + 1, :]
            h2 = AA[level, k, planes + p : planes + p + 1, :]
            f0 = (next_axial(a2, h2) - a2) - (next_radial(a1) - a1)
            f1 = (next_radial(a0) - a0) - (b2 - a2)
            f2 = (b1 - a1) - (next_axial(a0, h0) - a0)
            for c, f in enumerate((f0, f1, f2)):
                value = G[c, p] * f - NS[k, c, p]
                I[level, k, c, p] = value
                if c != 1:
                    at = (0 if c == 0 else planes) + p
                    SI[level, k, at : at + 1, :] = value[rows - 1 : rows, :]
            if p == planes - 1:
                z_i(level, k).start()

        @pl.when(has_above)
        def _():
            ax_i(level, k).start()

    def curl(level, k):
        z_i(level, k).wait_recv()

        @pl.when(has_below)
        def _():
            ax_i(level, k).wait_recv()

        for p in range(planes):
            i0, i1, i2 = I[level, k, 0, p], I[level, k, 1, p], I[level, k, 2, p]
            if p > 0:
                b1, b2 = I[level, k, 1, p - 1], I[level, k, 2, p - 1]
            else:
                b1, b2 = ZI[level, k, 0], ZI[level, k, 1]
            h0 = AI[level, k, p : p + 1, :]
            h2 = AI[level, k, planes + p : planes + p + 1, :]
            c0 = (i2 - prev_axial(i2, h2)) - (i1 - prev_radial(i1))
            c1 = (i0 - prev_radial(i0)) - (i2 - b2)
            c2 = (i1 - b1) - (i0 - prev_axial(i0, h0))
            for c, value in enumerate((c0, c1, c2)):
                field = X[level, k, c, p]
                r = -value - mass_term * field
                if level == 0:
                    d = r * (1.0 / cheb_centre)
                    D0[k, c, p] = d
                    X[1, k, c, p] = field + d
                elif level == 1:
                    d = (rho_second * rho_first) * D0[k, c, p] + (2.0 * rho_second / cheb_halfwidth) * r
                    X[2, k, c, p] = field + d
                else:
                    RS[k, c, p] = r
        if level < 2:
            send_a(level + 1, k)
        if level > 0:
            out_away(level - 1, k).start()
            out_here(level - 1, k).start()

    def stage(s, k):
        if s == 0:
            @pl.when(k == 0)
            def _():
                local_in().wait()

            swap_in(k).wait_recv()
            send_a(0, k)
        elif s == 1:
            @pl.when(k == 0)
            def _():
                for step in range(1, n_az):
                    give_pieces(step).wait_recv()
                own = smap[...]

                for c in range(3):
                    def add(p, total, c=c):
                        for q in range(slots):
                            total = total + jnp.where(own == p * slots + q, PG[p, c, q : q + 1, :], 0.0)
                        return total

                    TAB[c] = lax.fori_loop(0, n_az, add, jnp.zeros(own.shape, F32))
                swap_g().wait_recv()

            sources(k)
            intensity(0, k)
        elif s % 2 == 0:
            curl(s // 2 - 1, k)
        else:
            intensity(s // 2, k)

    stages = 1 + 2 * LEVELS

    def wave(t, carry):
        for s in reversed(range(stages)):
            chunk = t - s

            @pl.when(jnp.logical_and(chunk >= 0, chunk < half // GROUP))
            def _(s=s, chunk=chunk):
                def one(d, inner):
                    stage(s, chunk * GROUP + d)
                    return inner

                lax.fori_loop(0, GROUP, one, 0)

        return carry

    lax.fori_loop(0, half // GROUP + stages - 1, wave, 0)

    for step in range(1, n_az):
        give_pieces(step).wait_send()
    swap_g().wait_send()

    def finish(k, carry):
        swap_in(k).wait_send()
        for level in range(LEVELS):
            z_a(level, k).wait_send()
            z_i(level, k).wait_send()

            @pl.when(has_below)
            def _():
                ax_a(level, k).wait_send()

            @pl.when(has_above)
            def _():
                ax_i(level, k).wait_send()

        for which in range(2):
            out_here(which, k).wait()
            out_away(which, k).wait()
        return carry

    lax.fori_loop(0, half, finish, 0)


def shards(n_az, n_ax, start_field, reluctivity, lamination, magnets, region_ids, pieces, slot_map):
    devs, comps, cells, rows, radial = start_field.shape
    slots = pieces.shape[2]
    half, planes = devs // 2, 2 * cells
    by_slot = jnp.transpose(pieces, (0, 2, 1))
    base = lax.axis_index("az") // 2 * (2 * slots)
    own = lax.dynamic_slice_in_dim(slot_map, base, 2 * slots, 1).T

    tile = (rows, radial)
    dma = pltpu.SemaphoreType.DMA
    phase = (LEVELS, half)
    anywhere = pl.BlockSpec(memory_space=pl.ANY)
    block = (half, comps, planes) + tile
    shape = jax.ShapeDtypeStruct(start_field.shape, F32)
    return pl.pallas_call(
        functools.partial(kernel, n_az, n_ax, devs, cells, slots),
        out_shape=(shape, shape),
        in_specs=[anywhere] * 7,
        out_specs=(anywhere, anywhere),
        scratch_shapes=[
            pltpu.VMEM(reluctivity.shape, F32),
            pltpu.VMEM(lamination.shape, jnp.int32),
            pltpu.VMEM(lamination.shape, jnp.int32),
            pltpu.VMEM(lamination.shape, jnp.int32),
            pltpu.VMEM(by_slot.shape, F32),
            pltpu.VMEM(own.shape, jnp.int32),
            pltpu.VMEM((LEVELS,) + block, F32),
            pltpu.VMEM(block, F32),
            pltpu.VMEM((LEVELS,) + block, F32),
            pltpu.VMEM(block, F32),
            pltpu.VMEM(block, F32),
            pltpu.VMEM((comps + 1, planes) + tile, F32),
            pltpu.VMEM((n_az,) + by_slot.shape, F32),
            pltpu.VMEM((comps,) + own.shape, F32),
            pltpu.VMEM(phase + (2,) + tile, F32),
            pltpu.VMEM(phase + (2,) + tile, F32),
        ]
        + [pltpu.VMEM(phase + (2 * planes, radial), F32)] * 4
        + [dma((6,)), dma, dma((half,)), dma((half,)), dma, dma, dma((n_az,)), dma((n_az,))]
        + [dma(phase)] * 8
        + [dma((2, half))] * 3,
        compiler_params=pltpu.CompilerParams(
            collective_id=0, has_side_effects=True, vmem_limit_bytes=60 * 1024 * 1024
        ),
        cost_estimate=pl.CostEstimate(
            flops=150 * start_field.size, bytes_accessed=12 * start_field.size, transcendentals=0
        ),
    )(start_field, reluctivity, lamination, magnets, region_ids, by_slot, own)


def solution(mesh):
    placed = (
        P(None, None, "az", "ax", None),
        P(None, "az", "ax", None),
        P("az", "ax", None),
        P("az", "ax", None),
        P("az", "ax", None),
        P(None, None, "az"),
        P(),
    )
    return jax.shard_map(
        functools.partial(shards, mesh.shape["az"], mesh.shape["ax"]),
        mesh=mesh,
        in_specs=placed,
        out_specs=(P(None, None, "az", "ax", None), P(None, None, "az", "ax", None)),
        check_vma=False,
    )
```

```python
import functools

import jax
import jax.numpy as jnp
from jax import lax
from jax.experimental import pallas as pl
from jax.experimental.pallas import tpu as pltpu
from jax.sharding import PartitionSpec as P

mass_term = 1.0
cheb_centre = 8.5
cheb_halfwidth = 7.5
cheb_sigma = cheb_centre / cheb_halfwidth
rho_first = 1.0 / cheb_sigma
rho_second = 1.0 / (2.0 * cheb_sigma - rho_first)

MESH = pl.DeviceIdType.MESH
F32 = jnp.float32
LEVELS = 3
GROUP = 2
AHEAD = 2


def kernel(
    n_az, n_ax, devs, cells, slots,
    start, rel_in, lam_in, mag_in, reg_in, pcs_in, smap_in,
    sol, res,
    rel, lam, mag, reg, pcs, smap,
    X, D0, I, NS, RS, G, PG, TAB, ZA, ZI, AA, AI, SA, SI,
    ops, in_loc, in_s, in_r, g_s, g_r, p_s, p_r,
    za_s, za_r, zi_s, zi_r, aa_s, aa_r, ai_s, ai_r, o_s, o_r, o_l,
):
    half = devs // 2
    planes = 2 * cells
    rows, radial = X.shape[-2], X.shape[-1]
    az, ax = lax.axis_index("az"), lax.axis_index("ax")
    side = lax.rem(az, 2)
    partner = az + 1 - 2 * side
    up, down = lax.rem(az + 2, n_az), lax.rem(az + n_az - 2, n_az)
    mine = pl.ds(cells * side, cells)
    theirs = pl.ds(cells * (1 - side), cells)
    has_below, has_above = ax > 0, ax < n_ax - 1

    def remote(src, dst, s, r, where):
        return pltpu.make_async_remote_copy(
            src_ref=src, dst_ref=dst, send_sem=s, recv_sem=r, device_id=where, device_id_type=MESH
        )

    def local_in():
        return pltpu.make_async_copy(start.at[pl.ds(half * side, half)], X.at[0, :, :, mine], in_loc)

    def swap_in(k):
        return remote(
            start.at[half * (1 - side) + k], X.at[0, k, :, mine], in_s.at[k], in_r.at[k], {"az": partner}
        )

    def swap_g():
        return remote(G.at[:, mine], G.at[:, mine], g_s, g_r, {"az": partner})

    def give_pieces(step):
        return remote(PG.at[az], PG.at[az], p_s.at[step], p_r.at[step], {"az": lax.rem(az + step, n_az)})

    def z_a(level, k):
        return remote(
            X.at[level, k, 1:3, 0], ZA.at[level, k], za_s.at[level, k], za_r.at[level, k], {"az": down}
        )

    def z_i(level, k):
        return remote(
            I.at[level, k, 1:3, planes - 1], ZI.at[level, k], zi_s.at[level, k], zi_r.at[level, k], {"az": up}
        )

    def ax_a(level, k):
        return remote(SA.at[level, k], AA.at[level, k], aa_s.at[level, k], aa_r.at[level, k], {"ax": ax - 1})

    def ax_i(level, k):
        return remote(SI.at[level, k], AI.at[level, k], ai_s.at[level, k], ai_r.at[level, k], {"ax": ax + 1})

    def out_away(which, k):
        src, dst = ((X.at[2, k], sol), (RS.at[k], res))[which]
        return remote(
            src.at[:, theirs], dst.at[half * side + k], o_s.at[which, k], o_r.at[which, k], {"az": partner}
        )

    def out_here(which, k):
        src, dst = ((X.at[2, k], sol), (RS.at[k], res))[which]
        return pltpu.make_async_copy(src.at[:, mine], dst.at[half * side + k], o_l.at[which, k])

    operands = [
        pltpu.make_async_copy(src, dst, ops.at[j])
        for j, (src, dst) in enumerate(
            ((rel_in, rel), (lam_in, lam), (mag_in, mag), (reg_in, reg), (pcs_in, pcs), (smap_in, smap))
        )
    ]
    for copy in operands:
        copy.start()
    local_in().start()
    barrier = pltpu.get_barrier_semaphore()
    for step in range(1, n_az):
        pl.semaphore_signal(
            barrier, inc=1, device_id={"az": lax.rem(az + step, n_az)}, device_id_type=MESH
        )

    @pl.when(has_below)
    def _():
        pl.semaphore_signal(barrier, inc=1, device_id={"ax": ax - 1}, device_id_type=MESH)

    @pl.when(has_above)
    def _():
        pl.semaphore_signal(barrier, inc=1, device_id={"ax": ax + 1}, device_id_type=MESH)

    for copy in operands:
        copy.wait()
    for p in range(cells):
        G[0, cells * side + p] = rel[0, p]
        G[1, cells * side + p] = rel[1, p] * (1.0 + 3.0 * lam[p].astype(F32))
        G[2, cells * side + p] = rel[2, p]
        G[3, cells * side + p] = jnp.where(mag[p] == 1, reg[p] - az * slots, -1).astype(F32)
    PG[az] = pcs[...]

    pl.semaphore_wait(barrier, n_az - 1 + has_below.astype(jnp.int32) + has_above.astype(jnp.int32))

    swap_in(0).start()
    for step in range(1, n_az):
        give_pieces(step).start()
    swap_g().start()

    for k in range(1, AHEAD):
        swap_in(k).start()

    @pl.when(jnp.logical_not(has_above))
    def _():
        AA[...] = jnp.zeros_like(AA)

    @pl.when(jnp.logical_not(has_below))
    def _():
        AI[...] = jnp.zeros_like(AI)

    row_of = lax.broadcasted_iota(jnp.int32, (rows, radial), 0)
    lane_of = lax.broadcasted_iota(jnp.int32, (rows, radial), 1)

    def next_radial(v):
        return jnp.where(lane_of == radial - 1, 0.0, pltpu.roll(v, radial - 1, 1))

    def prev_radial(v):
        return jnp.where(lane_of == 0, 0.0, pltpu.roll(v, 1, 1))

    def next_axial(v, halo):
        return jnp.where(row_of == rows - 1, halo, pltpu.roll(v, rows - 1, 0))

    def prev_axial(v, halo):
        return jnp.where(row_of == 0, halo, pltpu.roll(v, 1, 0))

    def send_a(level, k):
        z_a(level, k).start()
        for p in range(planes):
            for j, c in enumerate((0, 2)):
                SA[level, k, j * planes + p : j * planes + p + 1, :] = X[level, k, c, p, 0:1, :]

        @pl.when(has_below)
        def _():
            ax_a(level, k).start()

    def sources(k):
        table = TAB[...]
        lane = lax.broadcasted_iota(jnp.int32, table.shape[1:], 1)
        for c in range(3):
            column = jnp.sum(jnp.where(lane == half * side + k, table[c], 0.0), axis=1, keepdims=True)
            values = [jnp.broadcast_to(column[j : j + 1], (rows, radial)) for j in range(2 * slots)]
            for p in range(planes):
                code = G[3, p]
                total = jnp.zeros((rows, radial), F32)
                for j in range(slots):
                    total = jnp.where(code == float(j), values[p // cells * slots + j], total)
                NS[k, c, p] = G[c, p] * total

    def intensity(level, k):
        z_a(level, k).wait_recv()

        @pl.when(has_above)
        def _():
            ax_a(level, k).wait_recv()

        for p in reversed(range(planes)):
            a0, a1, a2 = X[level, k, 0, p], X[level, k, 1, p], X[level, k, 2, p]
            if p < planes - 1:
                b1, b2 = X[level, k, 1, p + 1], X[level, k, 2, p + 1]
            else:
                b1, b2 = ZA[level, k, 0], ZA[level, k, 1]
            h0 = AA[level, k, p : p + 1, :]
            h2 = AA[level, k, planes + p : planes + p + 1, :]
            f0 = (next_axial(a2, h2) - a2) - (next_radial(a1) - a1)
            f1 = (next_radial(a0) - a0) - (b2 - a2)
            f2 = (b1 - a1) - (next_axial(a0, h0) - a0)
            for c, f in enumerate((f0, f1, f2)):
                value = G[c, p] * f - NS[k, c, p]
                I[level, k, c, p] = value
                if c != 1:
                    at = (0 if c == 0 else planes) + p
                    SI[level, k, at : at + 1, :] = value[rows - 1 : rows, :]
            if p == planes - 1:
                z_i(level, k).start()

        @pl.when(has_above)
        def _():
            ax_i(level, k).start()

    def curl(level, k):
        z_i(level, k).wait_recv()

        @pl.when(has_below)
        def _():
            ax_i(level, k).wait_recv()

        for p in range(planes):
            i0, i1, i2 = I[level, k, 0, p], I[level, k, 1, p], I[level, k, 2, p]
            if p > 0:
                b1, b2 = I[level, k, 1, p - 1], I[level, k, 2, p - 1]
            else:
                b1, b2 = ZI[level, k, 0], ZI[level, k, 1]
            h0 = AI[level, k, p : p + 1, :]
            h2 = AI[level, k, planes + p : planes + p + 1, :]
            c0 = (i2 - prev_axial(i2, h2)) - (i1 - prev_radial(i1))
            c1 = (i0 - prev_radial(i0)) - (i2 - b2)
            c2 = (i1 - b1) - (i0 - prev_axial(i0, h0))
            for c, value in enumerate((c0, c1, c2)):
                field = X[level, k, c, p]
                r = -value - mass_term * field
                if level == 0:
                    d = r * (1.0 / cheb_centre)
                    D0[k, c, p] = d
                    X[1, k, c, p] = field + d
                elif level == 1:
                    d = (rho_second * rho_first) * D0[k, c, p] + (2.0 * rho_second / cheb_halfwidth) * r
                    X[2, k, c, p] = field + d
                else:
                    RS[k, c, p] = r
        if level < 2:
            send_a(level + 1, k)
        if level > 0:
            out_away(level - 1, k).start()
            out_here(level - 1, k).start()

    def stage(s, k):
        if s == 0:
            @pl.when(k == 0)
            def _():
                local_in().wait()

            swap_in(k).wait_recv()

            @pl.when(k + AHEAD < half)
            def _():
                swap_in(k + AHEAD).start()

            send_a(0, k)
        elif s == 1:
            @pl.when(k == 0)
            def _():
                for step in range(1, n_az):
                    give_pieces(step).wait_recv()
                own = smap[...]

                for c in range(3):
                    def add(p, total, c=c):
                        for q in range(slots):
                            total = total + jnp.where(own == p * slots + q, PG[p, c, q : q + 1, :], 0.0)
                        return total

                    TAB[c] = lax.fori_loop(0, n_az, add, jnp.zeros(own.shape, F32))
                swap_g().wait_recv()

            sources(k)
            intensity(0, k)
        elif s % 2 == 0:
            curl(s // 2 - 1, k)
        else:
            intensity(s // 2, k)

    stages = 1 + 2 * LEVELS

    def wave(t, carry):
        for s in reversed(range(stages)):
            chunk = t - s

            @pl.when(jnp.logical_and(chunk >= 0, chunk < half // GROUP))
            def _(s=s, chunk=chunk):
                def one(d, inner):
                    stage(s, chunk * GROUP + d)
                    return inner

                lax.fori_loop(0, GROUP, one, 0)

        return carry

    lax.fori_loop(0, half // GROUP + stages - 1, wave, 0)

    for step in range(1, n_az):
        give_pieces(step).wait_send()
    swap_g().wait_send()

    def finish(k, carry):
        swap_in(k).wait_send()
        for level in range(LEVELS):
            z_a(level, k).wait_send()
            z_i(level, k).wait_send()

            @pl.when(has_below)
            def _():
                ax_a(level, k).wait_send()

            @pl.when(has_above)
            def _():
                ax_i(level, k).wait_send()

        for which in range(2):
            out_here(which, k).wait()
            out_away(which, k).wait()
        return carry

    lax.fori_loop(0, half, finish, 0)


def shards(n_az, n_ax, start_field, reluctivity, lamination, magnets, region_ids, pieces, slot_map):
    devs, comps, cells, rows, radial = start_field.shape
    slots = pieces.shape[2]
    half, planes = devs // 2, 2 * cells
    by_slot = jnp.transpose(pieces, (0, 2, 1))
    base = lax.axis_index("az") // 2 * (2 * slots)
    own = lax.dynamic_slice_in_dim(slot_map, base, 2 * slots, 1).T

    tile = (rows, radial)
    dma = pltpu.SemaphoreType.DMA
    phase = (LEVELS, half)
    anywhere = pl.BlockSpec(memory_space=pl.ANY)
    block = (half, comps, planes) + tile
    shape = jax.ShapeDtypeStruct(start_field.shape, F32)
    return pl.pallas_call(
        functools.partial(kernel, n_az, n_ax, devs, cells, slots),
        out_shape=(shape, shape),
        in_specs=[anywhere] * 7,
        out_specs=(anywhere, anywhere),
        scratch_shapes=[
            pltpu.VMEM(reluctivity.shape, F32),
            pltpu.VMEM(lamination.shape, jnp.int32),
            pltpu.VMEM(lamination.shape, jnp.int32),
            pltpu.VMEM(lamination.shape, jnp.int32),
            pltpu.VMEM(by_slot.shape, F32),
            pltpu.VMEM(own.shape, jnp.int32),
            pltpu.VMEM((LEVELS,) + block, F32),
            pltpu.VMEM(block, F32),
            pltpu.VMEM((LEVELS,) + block, F32),
            pltpu.VMEM(block, F32),
            pltpu.VMEM(block, F32),
            pltpu.VMEM((comps + 1, planes) + tile, F32),
            pltpu.VMEM((n_az,) + by_slot.shape, F32),
            pltpu.VMEM((comps,) + own.shape, F32),
            pltpu.VMEM(phase + (2,) + tile, F32),
            pltpu.VMEM(phase + (2,) + tile, F32),
        ]
        + [pltpu.VMEM(phase + (2 * planes, radial), F32)] * 4
        + [dma((6,)), dma, dma((half,)), dma((half,)), dma, dma, dma((n_az,)), dma((n_az,))]
        + [dma(phase)] * 8
        + [dma((2, half))] * 3,
        compiler_params=pltpu.CompilerParams(
            collective_id=0, has_side_effects=True, vmem_limit_bytes=60 * 1024 * 1024
        ),
        cost_estimate=pl.CostEstimate(
            flops=150 * start_field.size, bytes_accessed=12 * start_field.size, transcendentals=0
        ),
    )(start_field, reluctivity, lamination, magnets, region_ids, by_slot, own)


def solution(mesh):
    placed = (
        P(None, None, "az", "ax", None),
        P(None, "az", "ax", None),
        P("az", "ax", None),
        P("az", "ax", None),
        P("az", "ax", None),
        P(None, None, "az"),
        P(),
    )
    return jax.shard_map(
        functools.partial(shards, mesh.shape["az"], mesh.shape["ax"]),
        mesh=mesh,
        in_specs=placed,
        out_specs=(P(None, None, "az", "ax", None), P(None, None, "az", "ax", None)),
        check_vma=False,
    )
```

```python
import functools

import jax
import jax.numpy as jnp
from jax import lax
from jax.experimental import pallas as pl
from jax.experimental.pallas import tpu as pltpu
from jax.sharding import PartitionSpec as P

mass_term = 1.0
cheb_centre = 8.5
cheb_halfwidth = 7.5
cheb_sigma = cheb_centre / cheb_halfwidth
rho_first = 1.0 / cheb_sigma
rho_second = 1.0 / (2.0 * cheb_sigma - rho_first)

MESH = pl.DeviceIdType.MESH
F32 = jnp.float32
LEVELS = 3
GROUP = 2
AHEAD = 3
PLAIN = 2


def kernel(
    n_az, n_ax, devs, cells, slots,
    start, rel_in, lam_in, mag_in, reg_in, pcs_in, smap_in,
    sol, res,
    rel, lam, mag, reg, pcs, smap,
    X, D0, I, NS, RS, G, PG, TAB, ZA, ZI, AA, AI, SA, SI,
    XF, IF, RF, HA, HI, FA, FI, SFA, SFI,
    ops, in_loc, in_s, in_r, g_s, g_r, p_s, p_r,
    za_s, za_r, zi_s, zi_r, aa_s, aa_r, ai_s, ai_r, o_l, f_l, o_s, o_r,
    xf_s, xf_r, ha_s, ha_r, hi_s, hi_r, fa_s, fa_r, fi_s, fi_r,
):
    half = devs // 2
    short = half - PLAIN
    planes = 2 * cells
    rows, radial = X.shape[-2], X.shape[-1]
    az, ax = lax.axis_index("az"), lax.axis_index("ax")
    side = lax.rem(az, 2)
    partner = az + 1 - 2 * side
    up, down = lax.rem(az + 2, n_az), lax.rem(az + n_az - 2, n_az)
    mine = pl.ds(cells * side, cells)
    theirs = pl.ds(cells * (1 - side), cells)
    has_below, has_above = ax > 0, ax < n_ax - 1

    def remote(src, dst, s, r, where):
        return pltpu.make_async_remote_copy(
            src_ref=src, dst_ref=dst, send_sem=s, recv_sem=r, device_id=where, device_id_type=MESH
        )

    def local_in():
        return pltpu.make_async_copy(start.at[pl.ds(half * side, half)], X.at[0, :, :, mine], in_loc)

    def swap_in(k):
        return remote(
            start.at[half * (1 - side) + k], X.at[0, k, :, mine], in_s.at[k], in_r.at[k], {"az": partner}
        )

    def swap_g():
        return remote(G.at[:, mine], G.at[:, mine], g_s, g_r, {"az": partner})

    def give_pieces(step):
        return remote(PG.at[az], PG.at[az], p_s.at[step], p_r.at[step], {"az": lax.rem(az + step, n_az)})

    def z_a(level, k):
        return remote(
            X.at[level, k, 1:3, 0], ZA.at[level, k], za_s.at[level, k], za_r.at[level, k], {"az": down}
        )

    def z_i(level, k):
        return remote(
            I.at[level, k, 1:3, planes - 1], ZI.at[level, k], zi_s.at[level, k], zi_r.at[level, k], {"az": up}
        )

    def ax_a(level, k):
        return remote(SA.at[level, k], AA.at[level, k], aa_s.at[level, k], aa_r.at[level, k], {"ax": ax - 1})

    def ax_i(level, k):
        return remote(SI.at[level, k], AI.at[level, k], ai_s.at[level, k], ai_r.at[level, k], {"ax": ax + 1})

    def out_here(which, k):
        src, dst = ((X.at[2, k], sol), (RS.at[k], res))[which]
        return pltpu.make_async_copy(src.at[:, mine], dst.at[half * side + k], o_l.at[which, k])

    def out_away(which, k):
        src, dst = ((X.at[2, k], sol), (RS.at[k], res))[which]
        return remote(
            src.at[:, theirs], dst.at[half * side + k], o_s.at[which, k], o_r.at[which, k], {"az": partner}
        )

    def out_foreign(which, k):
        src, dst = ((XF.at[k], sol), (RF.at[k], res))[which]
        return pltpu.make_async_copy(src, dst.at[half * (1 - side) + k], f_l.at[which, k])

    def hand_x(k):
        return remote(X.at[2, k, :, theirs], XF.at[k], xf_s.at[k], xf_r.at[k], {"az": partner})

    def hand_a(k, src):
        return remote(src, HA.at[k], ha_s.at[k], ha_r.at[k], {"az": partner})

    def hand_i(k, src):
        return remote(src, HI.at[k], hi_s.at[k], hi_r.at[k], {"az": partner})

    def far_a(k):
        return remote(SFA.at[k], FA.at[k], fa_s.at[k], fa_r.at[k], {"ax": ax - 1})

    def far_i(k):
        return remote(SFI.at[k], FI.at[k], fi_s.at[k], fi_r.at[k], {"ax": ax + 1})

    operands = [
        pltpu.make_async_copy(src, dst, ops.at[j])
        for j, (src, dst) in enumerate(
            ((rel_in, rel), (lam_in, lam), (mag_in, mag), (reg_in, reg), (pcs_in, pcs), (smap_in, smap))
        )
    ]
    for copy in operands:
        copy.start()
    local_in().start()
    barrier = pltpu.get_barrier_semaphore()
    for step in range(1, n_az):
        pl.semaphore_signal(
            barrier, inc=1, device_id={"az": lax.rem(az + step, n_az)}, device_id_type=MESH
        )

    @pl.when(has_below)
    def _():
        pl.semaphore_signal(barrier, inc=1, device_id={"ax": ax - 1}, device_id_type=MESH)

    @pl.when(has_above)
    def _():
        pl.semaphore_signal(barrier, inc=1, device_id={"ax": ax + 1}, device_id_type=MESH)

    for copy in operands:
        copy.wait()
    for p in range(cells):
        G[0, cells * side + p] = rel[0, p]
        G[1, cells * side + p] = rel[1, p] * (1.0 + 3.0 * lam[p].astype(F32))
        G[2, cells * side + p] = rel[2, p]
        G[3, cells * side + p] = jnp.where(mag[p] == 1, reg[p] - az * slots, -1).astype(F32)
    PG[az] = pcs[...]

    pl.semaphore_wait(barrier, n_az - 1 + has_below.astype(jnp.int32) + has_above.astype(jnp.int32))

    swap_in(0).start()
    for step in range(1, n_az):
        give_pieces(step).start()
    swap_g().start()

    for k in range(1, AHEAD):
        swap_in(k).start()

    @pl.when(jnp.logical_not(has_above))
    def _():
        AA[...] = jnp.zeros_like(AA)
        FA[...] = jnp.zeros_like(FA)

    @pl.when(jnp.logical_not(has_below))
    def _():
        AI[...] = jnp.zeros_like(AI)
        FI[...] = jnp.zeros_like(FI)

    row_of = lax.broadcasted_iota(jnp.int32, (rows, radial), 0)
    lane_of = lax.broadcasted_iota(jnp.int32, (rows, radial), 1)

    def next_radial(v):
        return jnp.where(lane_of == radial - 1, 0.0, pltpu.roll(v, radial - 1, 1))

    def prev_radial(v):
        return jnp.where(lane_of == 0, 0.0, pltpu.roll(v, 1, 1))

    def next_axial(v, halo):
        return jnp.where(row_of == rows - 1, halo, pltpu.roll(v, rows - 1, 0))

    def prev_axial(v, halo):
        return jnp.where(row_of == 0, halo, pltpu.roll(v, 1, 0))

    def flux_of(a0, a1, a2, b1, b2, h0, h2):
        return (
            (next_axial(a2, h2) - a2) - (next_radial(a1) - a1),
            (next_radial(a0) - a0) - (b2 - a2),
            (b1 - a1) - (next_axial(a0, h0) - a0),
        )

    def curl_of(i0, i1, i2, b1, b2, h0, h2):
        return (
            (i2 - prev_axial(i2, h2)) - (i1 - prev_radial(i1)),
            (i0 - prev_radial(i0)) - (i2 - b2),
            (i1 - b1) - (i0 - prev_axial(i0, h0)),
        )

    def send_a(level, k):
        z_a(level, k).start()
        for p in range(planes):
            for j, c in enumerate((0, 2)):
                SA[level, k, j * planes + p : j * planes + p + 1, :] = X[level, k, c, p, 0:1, :]

        @pl.when(has_below)
        def _():
            ax_a(level, k).start()

    def sources(k):
        table = TAB[...]
        lane = lax.broadcasted_iota(jnp.int32, table.shape[1:], 1)
        for c in range(3):
            column = jnp.sum(jnp.where(lane == half * side + k, table[c], 0.0), axis=1, keepdims=True)
            values = [jnp.broadcast_to(column[j : j + 1], (rows, radial)) for j in range(2 * slots)]
            for p in range(planes):
                code = G[3, p]
                total = jnp.zeros((rows, radial), F32)
                for j in range(slots):
                    total = jnp.where(code == float(j), values[p // cells * slots + j], total)
                NS[k, c, p] = G[c, p] * total

    def intensity(level, k):
        z_a(level, k).wait_recv()

        @pl.when(has_above)
        def _():
            ax_a(level, k).wait_recv()

        for p in reversed(range(planes)):
            a0, a1, a2 = X[level, k, 0, p], X[level, k, 1, p], X[level, k, 2, p]
            if p < planes - 1:
                b1, b2 = X[level, k, 1, p + 1], X[level, k, 2, p + 1]
            else:
                b1, b2 = ZA[level, k, 0], ZA[level, k, 1]
            h0 = AA[level, k, p : p + 1, :]
            h2 = AA[level, k, planes + p : planes + p + 1, :]
            flux = flux_of(a0, a1, a2, b1, b2, h0, h2)
            for c, f in enumerate(flux):
                value = G[c, p] * f - NS[k, c, p]
                I[level, k, c, p] = value
                if c != 1:
                    at = (0 if c == 0 else planes) + p
                    SI[level, k, at : at + 1, :] = value[rows - 1 : rows, :]
            if p == planes - 1:
                z_i(level, k).start()

        @pl.when(has_above)
        def _():
            ax_i(level, k).start()

    def curl(level, k):
        z_i(level, k).wait_recv()

        @pl.when(has_below)
        def _():
            ax_i(level, k).wait_recv()

        for p in range(planes):
            i0, i1, i2 = I[level, k, 0, p], I[level, k, 1, p], I[level, k, 2, p]
            if p > 0:
                b1, b2 = I[level, k, 1, p - 1], I[level, k, 2, p - 1]
            else:
                b1, b2 = ZI[level, k, 0], ZI[level, k, 1]
            h0 = AI[level, k, p : p + 1, :]
            h2 = AI[level, k, planes + p : planes + p + 1, :]
            turned = curl_of(i0, i1, i2, b1, b2, h0, h2)
            for c, value in enumerate(turned):
                field = X[level, k, c, p]
                r = -value - mass_term * field
                if level == 2:
                    RS[k, c, p] = r
                elif level == 0:
                    d = r * (1.0 / cheb_centre)
                    D0[k, c, p] = d
                    X[1, k, c, p] = field + d
                else:
                    d = (rho_second * rho_first) * D0[k, c, p] + (2.0 * rho_second / cheb_halfwidth) * r
                    X[2, k, c, p] = field + d
        if level == 2:
            out_away(1, k).start()
            out_here(1, k).start()
        else:
            send_a(level + 1, k)
        if level == 1:
            @pl.when(k < short)
            def _():
                hand_x(k).start()

            @pl.when(k >= short)
            def _():
                out_away(0, k).start()

            out_here(0, k).start()

    def hand_ahead(k):
        @pl.when(side == 0)
        def _():
            hand_a(k, ZA.at[2, k]).start()
            hand_i(k, I.at[2, k, 1:3, cells - 1]).start()

        @pl.when(side == 1)
        def _():
            hand_a(k, X.at[2, k, 1:3, cells]).start()

    def last_curl(k):
        z_i(2, k).wait_recv()

        @pl.when(side == 1)
        def _():
            hand_i(k, ZI.at[2, k]).start()

        @pl.when(has_below)
        def _():
            ax_i(2, k).wait_recv()

        for q in range(cells):
            p = cells * side + q
            i0, i1, i2 = I[2, k, 0, p], I[2, k, 1, p], I[2, k, 2, p]
            if q > 0:
                b1, b2 = I[2, k, 1, p - 1], I[2, k, 2, p - 1]
            else:
                b1 = jnp.where(side == 0, ZI[2, k, 0], I[2, k, 1, cells - 1])
                b2 = jnp.where(side == 0, ZI[2, k, 1], I[2, k, 2, cells - 1])
            h0, h2 = (
                jnp.where(side == 0, AI[2, k, at : at + 1, :], AI[2, k, at + cells : at + cells + 1, :])
                for at in (q, planes + q)
            )
            for c, value in enumerate(curl_of(i0, i1, i2, b1, b2, h0, h2)):
                RS[k, c, p] = -value - mass_term * X[2, k, c, p]
        out_here(1, k).start()

    def far_start(k):
        hand_x(k).wait_recv()
        out_foreign(0, k).start()
        for q in range(cells):
            for j, c in enumerate((0, 2)):
                SFA[k, j * cells + q : j * cells + q + 1, :] = XF[k, c, q, 0:1, :]

        @pl.when(has_below)
        def _():
            far_a(k).start()

    def far_intensity(k):
        hand_a(k, ZA.at[2, k]).wait_recv()

        @pl.when(has_above)
        def _():
            far_a(k).wait_recv()

        table = TAB[...]
        lane = lax.broadcasted_iota(jnp.int32, table.shape[1:], 1)
        for q in range(cells):
            p = cells * side + q
            a0, a1, a2 = XF[k, 0, q], XF[k, 1, q], XF[k, 2, q]
            if q < cells - 1:
                b1, b2 = XF[k, 1, q + 1], XF[k, 2, q + 1]
            else:
                b1, b2 = HA[k, 0], HA[k, 1]
            h0, h2 = FA[k, q : q + 1, :], FA[k, cells + q : cells + q + 1, :]
            code = G[3, p]
            for c, f in enumerate(flux_of(a0, a1, a2, b1, b2, h0, h2)):
                column = jnp.sum(
                    jnp.where(lane == half * (1 - side) + k, table[c], 0.0), axis=1, keepdims=True
                )
                total = jnp.zeros((rows, radial), F32)
                for j in range(slots):
                    own = jnp.where(side == 0, column[j : j + 1], column[slots + j : slots + j + 1])
                    total = jnp.where(code == float(j), jnp.broadcast_to(own, (rows, radial)), total)
                value = G[c, p] * (f - total)
                IF[k, c, q] = value
                if c != 1:
                    at = (0 if c == 0 else cells) + q
                    SFI[k, at : at + 1, :] = value[rows - 1 : rows, :]

        @pl.when(has_above)
        def _():
            far_i(k).start()

    def far_curl(k):
        hand_i(k, ZI.at[2, k]).wait_recv()

        @pl.when(has_below)
        def _():
            far_i(k).wait_recv()

        for q in range(cells):
            i0, i1, i2 = IF[k, 0, q], IF[k, 1, q], IF[k, 2, q]
            if q > 0:
                b1, b2 = IF[k, 1, q - 1], IF[k, 2, q - 1]
            else:
                b1, b2 = HI[k, 0], HI[k, 1]
            h0, h2 = FI[k, q : q + 1, :], FI[k, cells + q : cells + q + 1, :]
            for c, value in enumerate(curl_of(i0, i1, i2, b1, b2, h0, h2)):
                RF[k, c, q] = -value - mass_term * XF[k, c, q]
        out_foreign(1, k).start()

    def stage(s, k):
        if s == 0:
            @pl.when(k == 0)
            def _():
                local_in().wait()

            swap_in(k).wait_recv()

            @pl.when(k + AHEAD < half)
            def _():
                swap_in(k + AHEAD).start()

            send_a(0, k)
        elif s == 1:
            @pl.when(k == 0)
            def _():
                for step in range(1, n_az):
                    give_pieces(step).wait_recv()
                own = smap[...]

                for c in range(3):
                    def add(p, total, c=c):
                        for q in range(slots):
                            total = total + jnp.where(own == p * slots + q, PG[p, c, q : q + 1, :], 0.0)
                        return total

                    TAB[c] = lax.fori_loop(0, n_az, add, jnp.zeros(own.shape, F32))
                swap_g().wait_recv()

            sources(k)
            intensity(0, k)
        elif s == 5:
            intensity(2, k)

            @pl.when(k < short)
            def _():
                hand_ahead(k)
        elif s == 6:
            @pl.when(k < short)
            def _():
                last_curl(k)

            @pl.when(k >= short)
            def _():
                curl(2, k)
        elif s % 2 == 0:
            curl(s // 2 - 1, k)
        else:
            intensity(s // 2, k)

    def grouped(work, chunk, count):
        @pl.when(jnp.logical_and(chunk >= 0, chunk < count // GROUP))
        def _():
            def one(d, inner):
                work(chunk * GROUP + d)
                return inner

            lax.fori_loop(0, GROUP, one, 0)

    def wave(t, carry):
        for s in reversed(range(1 + 2 * LEVELS)):
            grouped(functools.partial(stage, s), t - s, half)
        for s, work in ((8, far_curl), (7, far_intensity), (6, far_start)):
            grouped(work, t - s, short)
        return carry

    lax.fori_loop(0, max(half // GROUP + 6, short // GROUP + 8), wave, 0)

    for step in range(1, n_az):
        give_pieces(step).wait_send()
    swap_g().wait_send()

    def finish(k, carry):
        swap_in(k).wait_send()
        for level in range(LEVELS):
            z_a(level, k).wait_send()
            z_i(level, k).wait_send()

            @pl.when(has_below)
            def _():
                ax_a(level, k).wait_send()

            @pl.when(has_above)
            def _():
                ax_i(level, k).wait_send()

        for which in range(2):
            out_here(which, k).wait()
        return carry

    lax.fori_loop(0, half, finish, 0)

    def finish_short(k, carry):
        hand_x(k).wait_send()
        hand_a(k, ZA.at[2, k]).wait_send()
        hand_i(k, ZI.at[2, k]).wait_send()

        @pl.when(has_below)
        def _():
            far_a(k).wait_send()

        @pl.when(has_above)
        def _():
            far_i(k).wait_send()

        for which in range(2):
            out_foreign(which, k).wait()
        return carry

    lax.fori_loop(0, short, finish_short, 0)

    def finish_plain(k, carry):
        for which in range(2):
            out_away(which, k).wait()
        return carry

    lax.fori_loop(short, half, finish_plain, 0)


def hand_over(a, b, a_out, b_out, sems):
    pieces = a.shape[0] // 4
    copies = [
        pltpu.make_async_copy(src.at[pl.ds(j * pieces, pieces)], dst.at[pl.ds(j * pieces, pieces)], sems.at[i, j])
        for i, (src, dst) in enumerate(((a, a_out), (b, b_out)))
        for j in range(4)
    ]
    for copy in copies:
        copy.start()
    for copy in copies:
        copy.wait()


def shards(n_az, n_ax, start_field, reluctivity, lamination, magnets, region_ids, pieces, slot_map):
    devs, comps, cells, rows, radial = start_field.shape
    slots = pieces.shape[2]
    half, planes = devs // 2, 2 * cells
    by_slot = jnp.transpose(pieces, (0, 2, 1))
    base = lax.axis_index("az") // 2 * (2 * slots)
    own = lax.dynamic_slice_in_dim(slot_map, base, 2 * slots, 1).T

    tile = (rows, radial)
    dma = pltpu.SemaphoreType.DMA
    phase = (LEVELS, half)
    anywhere = pl.BlockSpec(memory_space=pl.ANY)
    block = (half, comps, planes) + tile
    home = (half, comps, cells) + tile
    shape = jax.ShapeDtypeStruct(start_field.shape, F32)
    field, left = pl.pallas_call(
        functools.partial(kernel, n_az, n_ax, devs, cells, slots),
        out_shape=(shape, shape),
        in_specs=[anywhere] * 7,
        out_specs=(anywhere, anywhere),
        scratch_shapes=[
            pltpu.VMEM(reluctivity.shape, F32),
            pltpu.VMEM(lamination.shape, jnp.int32),
            pltpu.VMEM(lamination.shape, jnp.int32),
            pltpu.VMEM(lamination.shape, jnp.int32),
            pltpu.VMEM(by_slot.shape, F32),
            pltpu.VMEM(own.shape, jnp.int32),
            pltpu.VMEM((LEVELS,) + block, F32),
            pltpu.VMEM(block, F32),
            pltpu.VMEM((LEVELS,) + block, F32),
            pltpu.VMEM(block, F32),
            pltpu.VMEM(block, F32),
            pltpu.VMEM((comps + 1, planes) + tile, F32),
            pltpu.VMEM((n_az,) + by_slot.shape, F32),
            pltpu.VMEM((comps,) + own.shape, F32),
            pltpu.VMEM(phase + (2,) + tile, F32),
            pltpu.VMEM(phase + (2,) + tile, F32),
        ]
        + [pltpu.VMEM(phase + (2 * planes, radial), F32)] * 4
        + [pltpu.VMEM(home, F32)] * 3
        + [pltpu.VMEM((half, 2) + tile, F32)] * 2
        + [pltpu.VMEM((half, 2 * cells, radial), F32)] * 4
        + [dma((6,)), dma, dma((half,)), dma((half,)), dma, dma, dma((n_az,)), dma((n_az,))]
        + [dma(phase)] * 8
        + [dma((2, half))] * 4
        + [dma((half,))] * 10,
        compiler_params=pltpu.CompilerParams(
            collective_id=0, has_side_effects=True, vmem_limit_bytes=60 * 1024 * 1024
        ),
        cost_estimate=pl.CostEstimate(
            flops=150 * start_field.size, bytes_accessed=12 * start_field.size, transcendentals=0
        ),
    )(start_field, reluctivity, lamination, magnets, region_ids, by_slot, own)
    return pl.pallas_call(
        hand_over,
        out_shape=(shape, shape),
        in_specs=[anywhere] * 2,
        out_specs=(anywhere, anywhere),
        scratch_shapes=[dma((2, 4))],
        compiler_params=pltpu.CompilerParams(vmem_limit_bytes=60 * 1024 * 1024),
        cost_estimate=pl.CostEstimate(flops=0, bytes_accessed=16 * start_field.size, transcendentals=0),
    )(field, left)


def solution(mesh):
    placed = (
        P(None, None, "az", "ax", None),
        P(None, "az", "ax", None),
        P("az", "ax", None),
        P("az", "ax", None),
        P("az", "ax", None),
        P(None, None, "az"),
        P(),
    )
    return jax.shard_map(
        functools.partial(shards, mesh.shape["az"], mesh.shape["ax"]),
        mesh=mesh,
        in_specs=placed,
        out_specs=(P(None, None, "az", "ax", None), P(None, None, "az", "ax", None)),
        check_vma=False,
    )
```

```python
import functools

import jax
import jax.numpy as jnp
from jax import lax
from jax.experimental import pallas as pl
from jax.experimental.pallas import tpu as pltpu
from jax.sharding import PartitionSpec as P

mass_term = 1.0
cheb_centre = 8.5
cheb_halfwidth = 7.5
cheb_sigma = cheb_centre / cheb_halfwidth
rho_first = 1.0 / cheb_sigma
rho_second = 1.0 / (2.0 * cheb_sigma - rho_first)

MESH = pl.DeviceIdType.MESH
F32 = jnp.float32
LEVELS = 3
GROUP = 2
AHEAD = 3
PLAIN = 2


def kernel(
    n_az, n_ax, devs, cells, slots,
    start, rel_in, lam_in, mag_in, reg_in, pcs_in, smap_in,
    sol, res,
    rel, lam, mag, reg, pcs, smap, turned_map,
    X, D0, I, NS, RS, G, PG, TAB, ZA, ZI, AA, AI, SA, SI,
    XF, IF, RF, HA, HI, FA, FI, SFA, SFI,
    ops, in_loc, in_s, in_r, g_s, g_r, p_s, p_r,
    za_s, za_r, zi_s, zi_r, aa_s, aa_r, ai_s, ai_r, o_l, f_l, o_s, o_r,
    xf_s, xf_r, ha_s, ha_r, hi_s, hi_r, fa_s, fa_r, fi_s, fi_r,
):
    half = devs // 2
    short = half - PLAIN
    planes = 2 * cells
    rows, radial = X.shape[-2], X.shape[-1]
    az, ax = lax.axis_index("az"), lax.axis_index("ax")
    side = lax.rem(az, 2)
    partner = az + 1 - 2 * side
    up, down = lax.rem(az + 2, n_az), lax.rem(az + n_az - 2, n_az)
    mine = pl.ds(cells * side, cells)
    theirs = pl.ds(cells * (1 - side), cells)
    has_below, has_above = ax > 0, ax < n_ax - 1

    def remote(src, dst, s, r, where):
        return pltpu.make_async_remote_copy(
            src_ref=src, dst_ref=dst, send_sem=s, recv_sem=r, device_id=where, device_id_type=MESH
        )

    def local_in():
        return pltpu.make_async_copy(start.at[pl.ds(half * side, half)], X.at[0, :, :, mine], in_loc)

    def swap_in(k):
        return remote(
            start.at[half * (1 - side) + k], X.at[0, k, :, mine], in_s.at[k], in_r.at[k], {"az": partner}
        )

    def swap_g():
        return remote(G.at[:, mine], G.at[:, mine], g_s, g_r, {"az": partner})

    def give_pieces(step):
        return remote(PG.at[az], PG.at[az], p_s.at[step], p_r.at[step], {"az": lax.rem(az + step, n_az)})

    def z_a(level, k):
        return remote(
            X.at[level, k, 1:3, 0], ZA.at[level, k], za_s.at[level, k], za_r.at[level, k], {"az": down}
        )

    def z_i(level, k):
        return remote(
            I.at[level, k, 1:3, planes - 1], ZI.at[level, k], zi_s.at[level, k], zi_r.at[level, k], {"az": up}
        )

    def ax_a(level, k):
        return remote(SA.at[level, k], AA.at[level, k], aa_s.at[level, k], aa_r.at[level, k], {"ax": ax - 1})

    def ax_i(level, k):
        return remote(SI.at[level, k], AI.at[level, k], ai_s.at[level, k], ai_r.at[level, k], {"ax": ax + 1})

    def out_here(which, k):
        src, dst = ((X.at[2, k], sol), (RS.at[k], res))[which]
        return pltpu.make_async_copy(src.at[:, mine], dst.at[half * side + k], o_l.at[which, k])

    def out_away(which, k):
        src, dst = ((X.at[2, k], sol), (RS.at[k], res))[which]
        return remote(
            src.at[:, theirs], dst.at[half * side + k], o_s.at[which, k], o_r.at[which, k], {"az": partner}
        )

    def out_foreign(which, k):
        src, dst = ((XF.at[k], sol), (RF.at[k], res))[which]
        return pltpu.make_async_copy(src, dst.at[half * (1 - side) + k], f_l.at[which, k])

    def hand_x(k):
        return remote(X.at[2, k, :, theirs], XF.at[k], xf_s.at[k], xf_r.at[k], {"az": partner})

    def hand_a(k, src):
        return remote(src, HA.at[k], ha_s.at[k], ha_r.at[k], {"az": partner})

    def hand_i(k, src):
        return remote(src, HI.at[k], hi_s.at[k], hi_r.at[k], {"az": partner})

    def far_a(k):
        return remote(SFA.at[k], FA.at[k], fa_s.at[k], fa_r.at[k], {"ax": ax - 1})

    def far_i(k):
        return remote(SFI.at[k], FI.at[k], fi_s.at[k], fi_r.at[k], {"ax": ax + 1})

    operands = [
        pltpu.make_async_copy(src, dst, ops.at[j])
        for j, (src, dst) in enumerate(
            ((rel_in, rel), (lam_in, lam), (mag_in, mag), (reg_in, reg), (pcs_in, pcs), (smap_in, smap))
        )
    ]
    for copy in operands:
        copy.start()
    local_in().start()
    barrier = pltpu.get_barrier_semaphore()
    for step in range(1, n_az):
        pl.semaphore_signal(
            barrier, inc=1, device_id={"az": lax.rem(az + step, n_az)}, device_id_type=MESH
        )

    @pl.when(has_below)
    def _():
        pl.semaphore_signal(barrier, inc=1, device_id={"ax": ax - 1}, device_id_type=MESH)

    @pl.when(has_above)
    def _():
        pl.semaphore_signal(barrier, inc=1, device_id={"ax": ax + 1}, device_id_type=MESH)

    for copy in operands:
        copy.wait()
    for p in range(cells):
        G[0, cells * side + p] = rel[0, p]
        G[1, cells * side + p] = rel[1, p] * (1.0 + 3.0 * lam[p].astype(F32))
        G[2, cells * side + p] = rel[2, p]
        G[3, cells * side + p] = jnp.where(mag[p] == 1, reg[p] - az * slots, -1).astype(F32)
    PG[az] = pcs[...]

    pl.semaphore_wait(barrier, n_az - 1 + has_below.astype(jnp.int32) + has_above.astype(jnp.int32))

    swap_in(0).start()
    for step in range(1, n_az):
        give_pieces(step).start()
    swap_g().start()

    for k in range(1, AHEAD):
        swap_in(k).start()

    @pl.when(jnp.logical_not(has_above))
    def _():
        AA[...] = jnp.zeros_like(AA)
        FA[...] = jnp.zeros_like(FA)

    @pl.when(jnp.logical_not(has_below))
    def _():
        AI[...] = jnp.zeros_like(AI)
        FI[...] = jnp.zeros_like(FI)

    row_of = lax.broadcasted_iota(jnp.int32, (rows, radial), 0)
    lane_of = lax.broadcasted_iota(jnp.int32, (rows, radial), 1)

    def next_radial(v):
        return jnp.where(lane_of == radial - 1, 0.0, pltpu.roll(v, radial - 1, 1))

    def prev_radial(v):
        return jnp.where(lane_of == 0, 0.0, pltpu.roll(v, 1, 1))

    def next_axial(v, halo):
        return jnp.where(row_of == rows - 1, halo, pltpu.roll(v, rows - 1, 0))

    def prev_axial(v, halo):
        return jnp.where(row_of == 0, halo, pltpu.roll(v, 1, 0))

    def flux_of(a0, a1, a2, b1, b2, h0, h2):
        return (
            (next_axial(a2, h2) - a2) - (next_radial(a1) - a1),
            (next_radial(a0) - a0) - (b2 - a2),
            (b1 - a1) - (next_axial(a0, h0) - a0),
        )

    def curl_of(i0, i1, i2, b1, b2, h0, h2):
        return (
            (i2 - prev_axial(i2, h2)) - (i1 - prev_radial(i1)),
            (i0 - prev_radial(i0)) - (i2 - b2),
            (i1 - b1) - (i0 - prev_axial(i0, h0)),
        )

    def send_a(level, k):
        z_a(level, k).start()
        for p in range(planes):
            for j, c in enumerate((0, 2)):
                SA[level, k, j * planes + p : j * planes + p + 1, :] = X[level, k, c, p, 0:1, :]

        @pl.when(has_below)
        def _():
            ax_a(level, k).start()

    def sources(k):
        table = TAB[...]
        lane = lax.broadcasted_iota(jnp.int32, table.shape[1:], 1)
        for c in range(3):
            column = jnp.sum(jnp.where(lane == half * side + k, table[c], 0.0), axis=1, keepdims=True)
            values = [jnp.broadcast_to(column[j : j + 1], (rows, radial)) for j in range(2 * slots)]
            for p in range(planes):
                code = G[3, p]
                total = jnp.zeros((rows, radial), F32)
                for j in range(slots):
                    total = jnp.where(code == float(j), values[p // cells * slots + j], total)
                NS[k, c, p] = G[c, p] * total

    def intensity(level, k):
        z_a(level, k).wait_recv()

        @pl.when(has_above)
        def _():
            ax_a(level, k).wait_recv()

        for p in reversed(range(planes)):
            a0, a1, a2 = X[level, k, 0, p], X[level, k, 1, p], X[level, k, 2, p]
            if p < planes - 1:
                b1, b2 = X[level, k, 1, p + 1], X[level, k, 2, p + 1]
            else:
                b1, b2 = ZA[level, k, 0], ZA[level, k, 1]
            h0 = AA[level, k, p : p + 1, :]
            h2 = AA[level, k, planes + p : planes + p + 1, :]
            flux = flux_of(a0, a1, a2, b1, b2, h0, h2)
            for c, f in enumerate(flux):
                value = G[c, p] * f - NS[k, c, p]
                I[level, k, c, p] = value
                if c != 1:
                    at = (0 if c == 0 else planes) + p
                    SI[level, k, at : at + 1, :] = value[rows - 1 : rows, :]
            if p == planes - 1:
                z_i(level, k).start()

        @pl.when(has_above)
        def _():
            ax_i(level, k).start()

    def curl(level, k):
        z_i(level, k).wait_recv()

        @pl.when(has_below)
        def _():
            ax_i(level, k).wait_recv()

        for p in range(planes):
            i0, i1, i2 = I[level, k, 0, p], I[level, k, 1, p], I[level, k, 2, p]
            if p > 0:
                b1, b2 = I[level, k, 1, p - 1], I[level, k, 2, p - 1]
            else:
                b1, b2 = ZI[level, k, 0], ZI[level, k, 1]
            h0 = AI[level, k, p : p + 1, :]
            h2 = AI[level, k, planes + p : planes + p + 1, :]
            turned = curl_of(i0, i1, i2, b1, b2, h0, h2)
            for c, value in enumerate(turned):
                field = X[level, k, c, p]
                r = -value - mass_term * field
                if level == 2:
                    RS[k, c, p] = r
                elif level == 0:
                    d = r * (1.0 / cheb_centre)
                    D0[k, c, p] = d
                    X[1, k, c, p] = field + d
                else:
                    d = (rho_second * rho_first) * D0[k, c, p] + (2.0 * rho_second / cheb_halfwidth) * r
                    X[2, k, c, p] = field + d
        if level == 2:
            out_away(1, k).start()
            out_here(1, k).start()
        else:
            send_a(level + 1, k)
        if level == 1:
            @pl.when(k < short)
            def _():
                hand_x(k).start()

            @pl.when(k >= short)
            def _():
                out_away(0, k).start()

            out_here(0, k).start()

    def hand_ahead(k):
        @pl.when(side == 0)
        def _():
            hand_a(k, ZA.at[2, k]).start()
            hand_i(k, I.at[2, k, 1:3, cells - 1]).start()

        @pl.when(side == 1)
        def _():
            hand_a(k, X.at[2, k, 1:3, cells]).start()

    def last_curl(k):
        z_i(2, k).wait_recv()

        @pl.when(side == 1)
        def _():
            hand_i(k, ZI.at[2, k]).start()

        @pl.when(has_below)
        def _():
            ax_i(2, k).wait_recv()

        for q in range(cells):
            p = cells * side + q
            i0, i1, i2 = I[2, k, 0, p], I[2, k, 1, p], I[2, k, 2, p]
            if q > 0:
                b1, b2 = I[2, k, 1, p - 1], I[2, k, 2, p - 1]
            else:
                b1 = jnp.where(side == 0, ZI[2, k, 0], I[2, k, 1, cells - 1])
                b2 = jnp.where(side == 0, ZI[2, k, 1], I[2, k, 2, cells - 1])
            h0, h2 = (
                jnp.where(side == 0, AI[2, k, at : at + 1, :], AI[2, k, at + cells : at + cells + 1, :])
                for at in (q, planes + q)
            )
            for c, value in enumerate(curl_of(i0, i1, i2, b1, b2, h0, h2)):
                RS[k, c, p] = -value - mass_term * X[2, k, c, p]
        out_here(1, k).start()

    def far_start(k):
        hand_x(k).wait_recv()
        out_foreign(0, k).start()
        for q in range(cells):
            for j, c in enumerate((0, 2)):
                SFA[k, j * cells + q : j * cells + q + 1, :] = XF[k, c, q, 0:1, :]

        @pl.when(has_below)
        def _():
            far_a(k).start()

    def far_intensity(k):
        hand_a(k, ZA.at[2, k]).wait_recv()

        @pl.when(has_above)
        def _():
            far_a(k).wait_recv()

        table = TAB[...]
        lane = lax.broadcasted_iota(jnp.int32, table.shape[1:], 1)
        for q in range(cells):
            p = cells * side + q
            a0, a1, a2 = XF[k, 0, q], XF[k, 1, q], XF[k, 2, q]
            if q < cells - 1:
                b1, b2 = XF[k, 1, q + 1], XF[k, 2, q + 1]
            else:
                b1, b2 = HA[k, 0], HA[k, 1]
            h0, h2 = FA[k, q : q + 1, :], FA[k, cells + q : cells + q + 1, :]
            code = G[3, p]
            for c, f in enumerate(flux_of(a0, a1, a2, b1, b2, h0, h2)):
                column = jnp.sum(
                    jnp.where(lane == half * (1 - side) + k, table[c], 0.0), axis=1, keepdims=True
                )
                total = jnp.zeros((rows, radial), F32)
                for j in range(slots):
                    own = jnp.where(side == 0, column[j : j + 1], column[slots + j : slots + j + 1])
                    total = jnp.where(code == float(j), jnp.broadcast_to(own, (rows, radial)), total)
                value = G[c, p] * (f - total)
                IF[k, c, q] = value
                if c != 1:
                    at = (0 if c == 0 else cells) + q
                    SFI[k, at : at + 1, :] = value[rows - 1 : rows, :]

        @pl.when(has_above)
        def _():
            far_i(k).start()

    def far_curl(k):
        hand_i(k, ZI.at[2, k]).wait_recv()

        @pl.when(has_below)
        def _():
            far_i(k).wait_recv()

        for q in range(cells):
            i0, i1, i2 = IF[k, 0, q], IF[k, 1, q], IF[k, 2, q]
            if q > 0:
                b1, b2 = IF[k, 1, q - 1], IF[k, 2, q - 1]
            else:
                b1, b2 = HI[k, 0], HI[k, 1]
            h0, h2 = FI[k, q : q + 1, :], FI[k, cells + q : cells + q + 1, :]
            for c, value in enumerate(curl_of(i0, i1, i2, b1, b2, h0, h2)):
                RF[k, c, q] = -value - mass_term * XF[k, c, q]
        out_foreign(1, k).start()

    def stage(s, k):
        if s == 0:
            @pl.when(k == 0)
            def _():
                local_in().wait()

            swap_in(k).wait_recv()

            @pl.when(k + AHEAD < half)
            def _():
                swap_in(k + AHEAD).start()

            send_a(0, k)
        elif s == 1:
            @pl.when(k == 0)
            def _():
                for step in range(1, n_az):
                    give_pieces(step).wait_recv()
                turned_map[...] = jnp.zeros_like(turned_map)
                turned_map[0:devs, 0 : smap.shape[1]] = smap[...].astype(F32)
                turned_map[...] = jnp.transpose(turned_map[...])
                base = pl.multiple_of((az - side) * slots, 2 * slots)
                own = turned_map[pl.ds(base, 2 * slots), 0:devs]

                for c in range(3):
                    def add(p, total, c=c):
                        for q in range(slots):
                            total = total + jnp.where(own == (p * slots + q).astype(F32), PG[p, c, q : q + 1, :], 0.0)
                        return total

                    TAB[c] = lax.fori_loop(0, n_az, add, jnp.zeros(own.shape, F32))
                swap_g().wait_recv()

            sources(k)
            intensity(0, k)
        elif s == 5:
            intensity(2, k)

            @pl.when(k < short)
            def _():
                hand_ahead(k)
        elif s == 6:
            @pl.when(k < short)
            def _():
                last_curl(k)

            @pl.when(k >= short)
            def _():
                curl(2, k)
        elif s % 2 == 0:
            curl(s // 2 - 1, k)
        else:
            intensity(s // 2, k)

    def grouped(work, chunk, count):
        @pl.when(jnp.logical_and(chunk >= 0, chunk < count // GROUP))
        def _():
            def one(d, inner):
                work(chunk * GROUP + d)
                return inner

            lax.fori_loop(0, GROUP, one, 0)

    def wave(t, carry):
        for s in reversed(range(1 + 2 * LEVELS)):
            grouped(functools.partial(stage, s), t - s, half)
        for s, work in ((8, far_curl), (7, far_intensity), (6, far_start)):
            grouped(work, t - s, short)
        return carry

    lax.fori_loop(0, max(half // GROUP + 6, short // GROUP + 8), wave, 0)

    for step in range(1, n_az):
        give_pieces(step).wait_send()
    swap_g().wait_send()

    def finish(k, carry):
        swap_in(k).wait_send()
        for level in range(LEVELS):
            z_a(level, k).wait_send()
            z_i(level, k).wait_send()

            @pl.when(has_below)
            def _():
                ax_a(level, k).wait_send()

            @pl.when(has_above)
            def _():
                ax_i(level, k).wait_send()

        for which in range(2):
            out_here(which, k).wait()
        return carry

    lax.fori_loop(0, half, finish, 0)

    def finish_short(k, carry):
        hand_x(k).wait_send()
        hand_a(k, ZA.at[2, k]).wait_send()
        hand_i(k, ZI.at[2, k]).wait_send()

        @pl.when(has_below)
        def _():
            far_a(k).wait_send()

        @pl.when(has_above)
        def _():
            far_i(k).wait_send()

        for which in range(2):
            out_foreign(which, k).wait()
        return carry

    lax.fori_loop(0, short, finish_short, 0)

    def finish_plain(k, carry):
        for which in range(2):
            out_away(which, k).wait()
        return carry

    lax.fori_loop(short, half, finish_plain, 0)


def hand_over(a, b, a_out, b_out, held, in_sems, out_sems):
    parts = in_sems.shape[1]
    share = a.shape[0] // parts

    def pair(i, j):
        src, dst = ((a, a_out), (b, b_out))[i]
        rows = pl.ds(j * share, share)
        return (
            pltpu.make_async_copy(src.at[rows], held.at[i, rows], in_sems.at[i, j]),
            pltpu.make_async_copy(held.at[i, rows], dst.at[rows], out_sems.at[i, j]),
        )

    pairs = [pair(i, j) for j in range(parts) for i in range(2)]
    for first, _ in pairs:
        first.start()
    for first, second in pairs:
        first.wait()
        second.start()
    for _, second in pairs:
        second.wait()


def shards(n_az, n_ax, start_field, reluctivity, lamination, magnets, region_ids, pieces, slot_map):
    devs, comps, cells, rows, radial = start_field.shape
    slots = pieces.shape[2]
    half, planes = devs // 2, 2 * cells
    by_slot = jnp.transpose(pieces, (0, 2, 1))
    regions = slot_map.shape[1]
    square = -(-max(regions, devs) // 128) * 128

    tile = (rows, radial)
    dma = pltpu.SemaphoreType.DMA
    phase = (LEVELS, half)
    anywhere = pl.BlockSpec(memory_space=pl.ANY)
    block = (half, comps, planes) + tile
    home = (half, comps, cells) + tile
    shape = jax.ShapeDtypeStruct(start_field.shape, F32)
    field, left = pl.pallas_call(
        functools.partial(kernel, n_az, n_ax, devs, cells, slots),
        out_shape=(shape, shape),
        in_specs=[anywhere] * 7,
        out_specs=(anywhere, anywhere),
        scratch_shapes=[
            pltpu.VMEM(reluctivity.shape, F32),
            pltpu.VMEM(lamination.shape, jnp.int32),
            pltpu.VMEM(lamination.shape, jnp.int32),
            pltpu.VMEM(lamination.shape, jnp.int32),
            pltpu.VMEM(by_slot.shape, F32),
            pltpu.VMEM(slot_map.shape, jnp.int32),
            pltpu.VMEM((square, square), F32),
            pltpu.VMEM((LEVELS,) + block, F32),
            pltpu.VMEM(block, F32),
            pltpu.VMEM((LEVELS,) + block, F32),
            pltpu.VMEM(block, F32),
            pltpu.VMEM(block, F32),
            pltpu.VMEM((comps + 1, planes) + tile, F32),
            pltpu.VMEM((n_az,) + by_slot.shape, F32),
            pltpu.VMEM((comps, 2 * slots, devs), F32),
            pltpu.VMEM(phase + (2,) + tile, F32),
            pltpu.VMEM(phase + (2,) + tile, F32),
        ]
        + [pltpu.VMEM(phase + (2 * planes, radial), F32)] * 4
        + [pltpu.VMEM(home, F32)] * 3
        + [pltpu.VMEM((half, 2) + tile, F32)] * 2
        + [pltpu.VMEM((half, 2 * cells, radial), F32)] * 4
        + [dma((6,)), dma, dma((half,)), dma((half,)), dma, dma, dma((n_az,)), dma((n_az,))]
        + [dma(phase)] * 8
        + [dma((2, half))] * 4
        + [dma((half,))] * 10,
        compiler_params=pltpu.CompilerParams(
            collective_id=0, has_side_effects=True, vmem_limit_bytes=60 * 1024 * 1024
        ),
        cost_estimate=pl.CostEstimate(
            flops=150 * start_field.size, bytes_accessed=12 * start_field.size, transcendentals=0
        ),
    )(start_field, reluctivity, lamination, magnets, region_ids, by_slot, slot_map)
    return pl.pallas_call(
        hand_over,
        out_shape=(shape, shape),
        in_specs=[anywhere] * 2,
        out_specs=(anywhere, anywhere),
        scratch_shapes=[pltpu.VMEM((2,) + start_field.shape, F32), dma((2, 4)), dma((2, 4))],
        compiler_params=pltpu.CompilerParams(vmem_limit_bytes=60 * 1024 * 1024),
        cost_estimate=pl.CostEstimate(flops=0, bytes_accessed=16 * start_field.size, transcendentals=0),
    )(field, left)


def solution(mesh):
    placed = (
        P(None, None, "az", "ax", None),
        P(None, "az", "ax", None),
        P("az", "ax", None),
        P("az", "ax", None),
        P("az", "ax", None),
        P(None, None, "az"),
        P(),
    )
    return jax.shard_map(
        functools.partial(shards, mesh.shape["az"], mesh.shape["ax"]),
        mesh=mesh,
        in_specs=placed,
        out_specs=(P(None, None, "az", "ax", None), P(None, None, "az", "ax", None)),
        check_vma=False,
    )
```

```python
import functools

import jax
import jax.numpy as jnp
from jax import lax
from jax.experimental import pallas as pl
from jax.experimental.pallas import tpu as pltpu
from jax.sharding import PartitionSpec as P

mass_term = 1.0
cheb_centre = 8.5
cheb_halfwidth = 7.5
cheb_sigma = cheb_centre / cheb_halfwidth
rho_first = 1.0 / cheb_sigma
rho_second = 1.0 / (2.0 * cheb_sigma - rho_first)

MESH = pl.DeviceIdType.MESH
F32 = jnp.float32
LEVELS = 3
GROUP = 1
AHEAD = 3
PLAIN = 2


def kernel(
    n_az, n_ax, devs, cells, slots,
    start, rel_in, lam_in, mag_in, reg_in, pcs_in, smap_in,
    sol, res,
    rel, lam, mag, reg, pcs, smap, turned_map,
    X, D0, I, NS, RS, G, PG, TAB, ZA, ZI, AA, AI, SA, SI,
    XF, IF, RF, HA, HI, FA, FI, SFA, SFI,
    ops, in_loc, in_s, in_r, g_s, g_r, p_s, p_r,
    za_s, za_r, zi_s, zi_r, aa_s, aa_r, ai_s, ai_r, o_l, f_l, o_s, o_r,
    xf_s, xf_r, ha_s, ha_r, hi_s, hi_r, fa_s, fa_r, fi_s, fi_r,
):
    half = devs // 2
    short = half - PLAIN
    planes = 2 * cells
    rows, radial = X.shape[-2], X.shape[-1]
    az, ax = lax.axis_index("az"), lax.axis_index("ax")
    side = lax.rem(az, 2)
    partner = az + 1 - 2 * side
    up, down = lax.rem(az + 2, n_az), lax.rem(az + n_az - 2, n_az)
    mine = pl.ds(cells * side, cells)
    theirs = pl.ds(cells * (1 - side), cells)
    has_below, has_above = ax > 0, ax < n_ax - 1

    def remote(src, dst, s, r, where):
        return pltpu.make_async_remote_copy(
            src_ref=src, dst_ref=dst, send_sem=s, recv_sem=r, device_id=where, device_id_type=MESH
        )

    def local_in():
        return pltpu.make_async_copy(start.at[pl.ds(half * side, half)], X.at[0, :, :, mine], in_loc)

    def swap_in(k):
        return remote(
            start.at[half * (1 - side) + k], X.at[0, k, :, mine], in_s.at[k], in_r.at[k], {"az": partner}
        )

    def swap_g():
        return remote(G.at[:, mine], G.at[:, mine], g_s, g_r, {"az": partner})

    def give_pieces(step):
        return remote(PG.at[az], PG.at[az], p_s.at[step], p_r.at[step], {"az": lax.rem(az + step, n_az)})

    def z_a(level, k):
        return remote(
            X.at[level, k, 1:3, 0], ZA.at[level, k], za_s.at[level, k], za_r.at[level, k], {"az": down}
        )

    def z_i(level, k):
        return remote(
            I.at[level, k, 1:3, planes - 1], ZI.at[level, k], zi_s.at[level, k], zi_r.at[level, k], {"az": up}
        )

    def ax_a(level, k):
        return remote(SA.at[level, k], AA.at[level, k], aa_s.at[level, k], aa_r.at[level, k], {"ax": ax - 1})

    def ax_i(level, k):
        return remote(SI.at[level, k], AI.at[level, k], ai_s.at[level, k], ai_r.at[level, k], {"ax": ax + 1})

    def out_here(which, k):
        src, dst = ((X.at[2, k], sol), (RS.at[k], res))[which]
        return pltpu.make_async_copy(src.at[:, mine], dst.at[half * side + k], o_l.at[which, k])

    def out_away(which, k):
        src, dst = ((X.at[2, k], sol), (RS.at[k], res))[which]
        return remote(
            src.at[:, theirs], dst.at[half * side + k], o_s.at[which, k], o_r.at[which, k], {"az": partner}
        )

    def out_foreign(which, k):
        src, dst = ((XF.at[k], sol), (RF.at[k], res))[which]
        return pltpu.make_async_copy(src, dst.at[half * (1 - side) + k], f_l.at[which, k])

    def hand_x(k):
        return remote(X.at[2, k, :, theirs], XF.at[k], xf_s.at[k], xf_r.at[k], {"az": partner})

    def hand_a(k, src):
        return remote(src, HA.at[k], ha_s.at[k], ha_r.at[k], {"az": partner})

    def hand_i(k, src):
        return remote(src, HI.at[k], hi_s.at[k], hi_r.at[k], {"az": partner})

    def far_a(k):
        return remote(SFA.at[k], FA.at[k], fa_s.at[k], fa_r.at[k], {"ax": ax - 1})

    def far_i(k):
        return remote(SFI.at[k], FI.at[k], fi_s.at[k], fi_r.at[k], {"ax": ax + 1})

    operands = [
        pltpu.make_async_copy(src, dst, ops.at[j])
        for j, (src, dst) in enumerate(
            ((rel_in, rel), (lam_in, lam), (mag_in, mag), (reg_in, reg), (pcs_in, pcs), (smap_in, smap))
        )
    ]
    for copy in operands:
        copy.start()
    local_in().start()
    barrier = pltpu.get_barrier_semaphore()
    for step in range(1, n_az):
        pl.semaphore_signal(
            barrier, inc=1, device_id={"az": lax.rem(az + step, n_az)}, device_id_type=MESH
        )

    @pl.when(has_below)
    def _():
        pl.semaphore_signal(barrier, inc=1, device_id={"ax": ax - 1}, device_id_type=MESH)

    @pl.when(has_above)
    def _():
        pl.semaphore_signal(barrier, inc=1, device_id={"ax": ax + 1}, device_id_type=MESH)

    for copy in operands:
        copy.wait()
    for p in range(cells):
        G[0, cells * side + p] = rel[0, p]
        G[1, cells * side + p] = rel[1, p] * (1.0 + 3.0 * lam[p].astype(F32))
        G[2, cells * side + p] = rel[2, p]
        G[3, cells * side + p] = jnp.where(mag[p] == 1, reg[p] - az * slots, -1).astype(F32)
    PG[az] = pcs[...]

    pl.semaphore_wait(barrier, n_az - 1 + has_below.astype(jnp.int32) + has_above.astype(jnp.int32))

    swap_in(0).start()
    for step in range(1, n_az):
        give_pieces(step).start()
    swap_g().start()

    for k in range(1, AHEAD):
        swap_in(k).start()

    @pl.when(jnp.logical_not(has_above))
    def _():
        AA[...] = jnp.zeros_like(AA)
        FA[...] = jnp.zeros_like(FA)

    @pl.when(jnp.logical_not(has_below))
    def _():
        AI[...] = jnp.zeros_like(AI)
        FI[...] = jnp.zeros_like(FI)

    row_of = lax.broadcasted_iota(jnp.int32, (rows, radial), 0)
    lane_of = lax.broadcasted_iota(jnp.int32, (rows, radial), 1)

    def next_radial(v):
        return jnp.where(lane_of == radial - 1, 0.0, pltpu.roll(v, radial - 1, 1))

    def prev_radial(v):
        return jnp.where(lane_of == 0, 0.0, pltpu.roll(v, 1, 1))

    def next_axial(v, halo):
        return jnp.where(row_of == rows - 1, halo, pltpu.roll(v, rows - 1, 0))

    def prev_axial(v, halo):
        return jnp.where(row_of == 0, halo, pltpu.roll(v, 1, 0))

    def flux_of(a0, a1, a2, b1, b2, h0, h2):
        return (
            (next_axial(a2, h2) - a2) - (next_radial(a1) - a1),
            (next_radial(a0) - a0) - (b2 - a2),
            (b1 - a1) - (next_axial(a0, h0) - a0),
        )

    def curl_of(i0, i1, i2, b1, b2, h0, h2):
        return (
            (i2 - prev_axial(i2, h2)) - (i1 - prev_radial(i1)),
            (i0 - prev_radial(i0)) - (i2 - b2),
            (i1 - b1) - (i0 - prev_axial(i0, h0)),
        )

    def send_a(level, k):
        z_a(level, k).start()
        for p in range(planes):
            for j, c in enumerate((0, 2)):
                SA[level, k, j * planes + p : j * planes + p + 1, :] = X[level, k, c, p, 0:1, :]

        @pl.when(has_below)
        def _():
            ax_a(level, k).start()

    def sources(k):
        table = TAB[...]
        lane = lax.broadcasted_iota(jnp.int32, table.shape[1:], 1)
        for c in range(3):
            column = jnp.sum(jnp.where(lane == half * side + k, table[c], 0.0), axis=1, keepdims=True)
            values = [jnp.broadcast_to(column[j : j + 1], (rows, radial)) for j in range(2 * slots)]
            for p in range(planes):
                code = G[3, p]
                total = jnp.zeros((rows, radial), F32)
                for j in range(slots):
                    total = jnp.where(code == float(j), values[p // cells * slots + j], total)
                NS[k, c, p] = G[c, p] * total

    def intensity(level, k):
        z_a(level, k).wait_recv()

        @pl.when(has_above)
        def _():
            ax_a(level, k).wait_recv()

        for p in reversed(range(planes)):
            a0, a1, a2 = X[level, k, 0, p], X[level, k, 1, p], X[level, k, 2, p]
            if p < planes - 1:
                b1, b2 = X[level, k, 1, p + 1], X[level, k, 2, p + 1]
            else:
                b1, b2 = ZA[level, k, 0], ZA[level, k, 1]
            h0 = AA[level, k, p : p + 1, :]
            h2 = AA[level, k, planes + p : planes + p + 1, :]
            flux = flux_of(a0, a1, a2, b1, b2, h0, h2)
            for c, f in enumerate(flux):
                value = G[c, p] * f - NS[k, c, p]
                I[level, k, c, p] = value
                if c != 1:
                    at = (0 if c == 0 else planes) + p
                    SI[level, k, at : at + 1, :] = value[rows - 1 : rows, :]
            if p == planes - 1:
                z_i(level, k).start()

        @pl.when(has_above)
        def _():
            ax_i(level, k).start()

    def curl(level, k):
        z_i(level, k).wait_recv()

        @pl.when(has_below)
        def _():
            ax_i(level, k).wait_recv()

        for p in range(planes):
            i0, i1, i2 = I[level, k, 0, p], I[level, k, 1, p], I[level, k, 2, p]
            if p > 0:
                b1, b2 = I[level, k, 1, p - 1], I[level, k, 2, p - 1]
            else:
                b1, b2 = ZI[level, k, 0], ZI[level, k, 1]
            h0 = AI[level, k, p : p + 1, :]
            h2 = AI[level, k, planes + p : planes + p + 1, :]
            turned = curl_of(i0, i1, i2, b1, b2, h0, h2)
            for c, value in enumerate(turned):
                field = X[level, k, c, p]
                r = -value - mass_term * field
                if level == 2:
                    RS[k, c, p] = r
                elif level == 0:
                    d = r * (1.0 / cheb_centre)
                    D0[k, c, p] = d
                    X[1, k, c, p] = field + d
                else:
                    d = (rho_second * rho_first) * D0[k, c, p] + (2.0 * rho_second / cheb_halfwidth) * r
                    X[2, k, c, p] = field + d
        if level == 2:
            out_away(1, k).start()
            out_here(1, k).start()
        else:
            send_a(level + 1, k)
        if level == 1:
            @pl.when(k < short)
            def _():
                hand_x(k).start()

            @pl.when(k >= short)
            def _():
                out_away(0, k).start()

            out_here(0, k).start()

    def hand_ahead(k):
        @pl.when(side == 0)
        def _():
            hand_a(k, ZA.at[2, k]).start()
            hand_i(k, I.at[2, k, 1:3, cells - 1]).start()

        @pl.when(side == 1)
        def _():
            hand_a(k, X.at[2, k, 1:3, cells]).start()

    def last_curl(k):
        z_i(2, k).wait_recv()

        @pl.when(side == 1)
        def _():
            hand_i(k, ZI.at[2, k]).start()

        @pl.when(has_below)
        def _():
            ax_i(2, k).wait_recv()

        for q in range(cells):
            p = cells * side + q
            i0, i1, i2 = I[2, k, 0, p], I[2, k, 1, p], I[2, k, 2, p]
            if q > 0:
                b1, b2 = I[2, k, 1, p - 1], I[2, k, 2, p - 1]
            else:
                b1 = jnp.where(side == 0, ZI[2, k, 0], I[2, k, 1, cells - 1])
                b2 = jnp.where(side == 0, ZI[2, k, 1], I[2, k, 2, cells - 1])
            h0, h2 = (
                jnp.where(side == 0, AI[2, k, at : at + 1, :], AI[2, k, at + cells : at + cells + 1, :])
                for at in (q, planes + q)
            )
            for c, value in enumerate(curl_of(i0, i1, i2, b1, b2, h0, h2)):
                RS[k, c, p] = -value - mass_term * X[2, k, c, p]
        out_here(1, k).start()

    def far_start(k):
        hand_x(k).wait_recv()
        out_foreign(0, k).start()
        for q in range(cells):
            for j, c in enumerate((0, 2)):
                SFA[k, j * cells + q : j * cells + q + 1, :] = XF[k, c, q, 0:1, :]

        @pl.when(has_below)
        def _():
            far_a(k).start()

    def far_intensity(k):
        hand_a(k, ZA.at[2, k]).wait_recv()

        @pl.when(has_above)
        def _():
            far_a(k).wait_recv()

        table = TAB[...]
        lane = lax.broadcasted_iota(jnp.int32, table.shape[1:], 1)
        for q in range(cells):
            p = cells * side + q
            a0, a1, a2 = XF[k, 0, q], XF[k, 1, q], XF[k, 2, q]
            if q < cells - 1:
                b1, b2 = XF[k, 1, q + 1], XF[k, 2, q + 1]
            else:
                b1, b2 = HA[k, 0], HA[k, 1]
            h0, h2 = FA[k, q : q + 1, :], FA[k, cells + q : cells + q + 1, :]
            code = G[3, p]
            for c, f in enumerate(flux_of(a0, a1, a2, b1, b2, h0, h2)):
                column = jnp.sum(
                    jnp.where(lane == half * (1 - side) + k, table[c], 0.0), axis=1, keepdims=True
                )
                total = jnp.zeros((rows, radial), F32)
                for j in range(slots):
                    own = jnp.where(side == 0, column[j : j + 1], column[slots + j : slots + j + 1])
                    total = jnp.where(code == float(j), jnp.broadcast_to(own, (rows, radial)), total)
                value = G[c, p] * (f - total)
                IF[k, c, q] = value
                if c != 1:
                    at = (0 if c == 0 else cells) + q
                    SFI[k, at : at + 1, :] = value[rows - 1 : rows, :]

        @pl.when(has_above)
        def _():
            far_i(k).start()

    def far_curl(k):
        hand_i(k, ZI.at[2, k]).wait_recv()

        @pl.when(has_below)
        def _():
            far_i(k).wait_recv()

        for q in range(cells):
            i0, i1, i2 = IF[k, 0, q], IF[k, 1, q], IF[k, 2, q]
            if q > 0:
                b1, b2 = IF[k, 1, q - 1], IF[k, 2, q - 1]
            else:
                b1, b2 = HI[k, 0], HI[k, 1]
            h0, h2 = FI[k, q : q + 1, :], FI[k, cells + q : cells + q + 1, :]
            for c, value in enumerate(curl_of(i0, i1, i2, b1, b2, h0, h2)):
                RF[k, c, q] = -value - mass_term * XF[k, c, q]
        out_foreign(1, k).start()

    def stage(s, k):
        if s == 0:
            @pl.when(k == 0)
            def _():
                local_in().wait()

            swap_in(k).wait_recv()

            @pl.when(k + AHEAD < half)
            def _():
                swap_in(k + AHEAD).start()

            send_a(0, k)
        elif s == 1:
            @pl.when(k == 0)
            def _():
                for step in range(1, n_az):
                    give_pieces(step).wait_recv()
                turned_map[...] = jnp.zeros_like(turned_map)
                turned_map[0:devs, 0 : smap.shape[1]] = smap[...].astype(F32)
                turned_map[...] = jnp.transpose(turned_map[...])
                base = pl.multiple_of((az - side) * slots, 2 * slots)
                own = turned_map[pl.ds(base, 2 * slots), 0:devs]

                for c in range(3):
                    def add(p, total, c=c):
                        for q in range(slots):
                            total = total + jnp.where(own == (p * slots + q).astype(F32), PG[p, c, q : q + 1, :], 0.0)
                        return total

                    TAB[c] = lax.fori_loop(0, n_az, add, jnp.zeros(own.shape, F32))
                swap_g().wait_recv()

            sources(k)
            intensity(0, k)
        elif s == 5:
            intensity(2, k)

            @pl.when(k < short)
            def _():
                hand_ahead(k)
        elif s == 6:
            @pl.when(k < short)
            def _():
                last_curl(k)

            @pl.when(k >= short)
            def _():
                curl(2, k)
        elif s % 2 == 0:
            curl(s // 2 - 1, k)
        else:
            intensity(s // 2, k)

    def grouped(work, chunk, count):
        @pl.when(jnp.logical_and(chunk >= 0, chunk < count // GROUP))
        def _():
            def one(d, inner):
                work(chunk * GROUP + d)
                return inner

            lax.fori_loop(0, GROUP, one, 0)

    def wave(t, carry):
        for s in reversed(range(1 + 2 * LEVELS)):
            grouped(functools.partial(stage, s), t - s, half)
        for s, work in ((9, far_curl), (8, far_intensity), (7, far_start)):
            grouped(work, t - s, short)
        return carry

    lax.fori_loop(0, max(half // GROUP + 6, short // GROUP + 9), wave, 0)

    for step in range(1, n_az):
        give_pieces(step).wait_send()
    swap_g().wait_send()

    def finish(k, carry):
        swap_in(k).wait_send()
        for level in range(LEVELS):
            z_a(level, k).wait_send()
            z_i(level, k).wait_send()

            @pl.when(has_below)
            def _():
                ax_a(level, k).wait_send()

            @pl.when(has_above)
            def _():
                ax_i(level, k).wait_send()

        for which in range(2):
            out_here(which, k).wait()
        return carry

    lax.fori_loop(0, half, finish, 0)

    def finish_short(k, carry):
        hand_x(k).wait_send()
        hand_a(k, ZA.at[2, k]).wait_send()
        hand_i(k, ZI.at[2, k]).wait_send()

        @pl.when(has_below)
        def _():
            far_a(k).wait_send()

        @pl.when(has_above)
        def _():
            far_i(k).wait_send()

        for which in range(2):
            out_foreign(which, k).wait()
        return carry

    lax.fori_loop(0, short, finish_short, 0)

    def finish_plain(k, carry):
        for which in range(2):
            out_away(which, k).wait()
        return carry

    lax.fori_loop(short, half, finish_plain, 0)


def hand_over(a, b, a_out, b_out, held, in_sems, out_sems):
    parts = in_sems.shape[1]
    share = a.shape[0] // parts

    def pair(i, j):
        src, dst = ((a, a_out), (b, b_out))[i]
        rows = pl.ds(j * share, share)
        return (
            pltpu.make_async_copy(src.at[rows], held.at[i, rows], in_sems.at[i, j]),
            pltpu.make_async_copy(held.at[i, rows], dst.at[rows], out_sems.at[i, j]),
        )

    pairs = [pair(i, j) for j in range(parts) for i in range(2)]
    for first, _ in pairs:
        first.start()
    for first, second in pairs:
        first.wait()
        second.start()
    for _, second in pairs:
        second.wait()


def shards(n_az, n_ax, start_field, reluctivity, lamination, magnets, region_ids, pieces, slot_map):
    devs, comps, cells, rows, radial = start_field.shape
    slots = pieces.shape[2]
    half, planes = devs // 2, 2 * cells
    by_slot = jnp.transpose(pieces, (0, 2, 1))
    regions = slot_map.shape[1]
    square = -(-max(regions, devs) // 128) * 128

    tile = (rows, radial)
    dma = pltpu.SemaphoreType.DMA
    phase = (LEVELS, half)
    anywhere = pl.BlockSpec(memory_space=pl.ANY)
    block = (half, comps, planes) + tile
    home = (half, comps, cells) + tile
    shape = jax.ShapeDtypeStruct(start_field.shape, F32)
    field, left = pl.pallas_call(
        functools.partial(kernel, n_az, n_ax, devs, cells, slots),
        out_shape=(shape, shape),
        in_specs=[anywhere] * 7,
        out_specs=(anywhere, anywhere),
        scratch_shapes=[
            pltpu.VMEM(reluctivity.shape, F32),
            pltpu.VMEM(lamination.shape, jnp.int32),
            pltpu.VMEM(lamination.shape, jnp.int32),
            pltpu.VMEM(lamination.shape, jnp.int32),
            pltpu.VMEM(by_slot.shape, F32),
            pltpu.VMEM(slot_map.shape, jnp.int32),
            pltpu.VMEM((square, square), F32),
            pltpu.VMEM((LEVELS,) + block, F32),
            pltpu.VMEM(block, F32),
            pltpu.VMEM((LEVELS,) + block, F32),
            pltpu.VMEM(block, F32),
            pltpu.VMEM(block, F32),
            pltpu.VMEM((comps + 1, planes) + tile, F32),
            pltpu.VMEM((n_az,) + by_slot.shape, F32),
            pltpu.VMEM((comps, 2 * slots, devs), F32),
            pltpu.VMEM(phase + (2,) + tile, F32),
            pltpu.VMEM(phase + (2,) + tile, F32),
        ]
        + [pltpu.VMEM(phase + (2 * planes, radial), F32)] * 4
        + [pltpu.VMEM(home, F32)] * 3
        + [pltpu.VMEM((half, 2) + tile, F32)] * 2
        + [pltpu.VMEM((half, 2 * cells, radial), F32)] * 4
        + [dma((6,)), dma, dma((half,)), dma((half,)), dma, dma, dma((n_az,)), dma((n_az,))]
        + [dma(phase)] * 8
        + [dma((2, half))] * 4
        + [dma((half,))] * 10,
        compiler_params=pltpu.CompilerParams(
            collective_id=0, has_side_effects=True, vmem_limit_bytes=60 * 1024 * 1024
        ),
        cost_estimate=pl.CostEstimate(
            flops=150 * start_field.size, bytes_accessed=12 * start_field.size, transcendentals=0
        ),
    )(start_field, reluctivity, lamination, magnets, region_ids, by_slot, slot_map)
    return pl.pallas_call(
        hand_over,
        out_shape=(shape, shape),
        in_specs=[anywhere] * 2,
        out_specs=(anywhere, anywhere),
        scratch_shapes=[pltpu.VMEM((2,) + start_field.shape, F32), dma((2, 4)), dma((2, 4))],
        compiler_params=pltpu.CompilerParams(vmem_limit_bytes=60 * 1024 * 1024),
        cost_estimate=pl.CostEstimate(flops=0, bytes_accessed=16 * start_field.size, transcendentals=0),
    )(field, left)


def solution(mesh):
    placed = (
        P(None, None, "az", "ax", None),
        P(None, "az", "ax", None),
        P("az", "ax", None),
        P("az", "ax", None),
        P("az", "ax", None),
        P(None, None, "az"),
        P(),
    )
    return jax.shard_map(
        functools.partial(shards, mesh.shape["az"], mesh.shape["ax"]),
        mesh=mesh,
        in_specs=placed,
        out_specs=(P(None, None, "az", "ax", None), P(None, None, "az", "ax", None)),
        check_vma=False,
    )
```

```python
import functools

import jax
import jax.numpy as jnp
from jax import lax
from jax.experimental import pallas as pl
from jax.experimental.pallas import tpu as pltpu
from jax.sharding import PartitionSpec as P

mass_term = 1.0
cheb_centre = 8.5
cheb_halfwidth = 7.5
cheb_sigma = cheb_centre / cheb_halfwidth
rho_first = 1.0 / cheb_sigma
rho_second = 1.0 / (2.0 * cheb_sigma - rho_first)

MESH = pl.DeviceIdType.MESH
F32 = jnp.float32
LEVELS = 3
GROUP = 4
AHEAD = 4
PLAIN = 4


def kernel(
    n_az, n_ax, devs, cells, slots,
    start, rel_in, lam_in, mag_in, reg_in, pcs_in, smap_in,
    sol, res,
    rel, lam, mag, reg, pcs, smap, turned_map,
    X, D0, I, NS, RS, G, PG, TAB, ZA, ZI, AA, AI, SA, SI,
    XF, IF, RF, HA, HI, FA, FI, SFA, SFI,
    ops, in_loc, in_s, in_r, g_s, g_r, p_s, p_r,
    za_s, za_r, zi_s, zi_r, aa_s, aa_r, ai_s, ai_r, o_l, f_l, o_s, o_r,
    xf_s, xf_r, ha_s, ha_r, hi_s, hi_r, fa_s, fa_r, fi_s, fi_r,
):
    half = devs // 2
    short = half - PLAIN
    planes = 2 * cells
    rows, radial = X.shape[-2], X.shape[-1]
    az, ax = lax.axis_index("az"), lax.axis_index("ax")
    side = lax.rem(az, 2)
    partner = az + 1 - 2 * side
    up, down = lax.rem(az + 2, n_az), lax.rem(az + n_az - 2, n_az)
    mine = pl.ds(cells * side, cells)
    theirs = pl.ds(cells * (1 - side), cells)
    has_below, has_above = ax > 0, ax < n_ax - 1

    def remote(src, dst, s, r, where):
        return pltpu.make_async_remote_copy(
            src_ref=src, dst_ref=dst, send_sem=s, recv_sem=r, device_id=where, device_id_type=MESH
        )

    def local_in():
        return pltpu.make_async_copy(start.at[pl.ds(half * side, half)], X.at[0, :, :, mine], in_loc)

    def swap_in(k):
        return remote(
            start.at[half * (1 - side) + k], X.at[0, k, :, mine], in_s.at[k], in_r.at[k], {"az": partner}
        )

    def swap_g():
        return remote(G.at[:, mine], G.at[:, mine], g_s, g_r, {"az": partner})

    def give_pieces(step):
        return remote(PG.at[az], PG.at[az], p_s.at[step], p_r.at[step], {"az": lax.rem(az + step, n_az)})

    def z_a(level, k):
        return remote(
            X.at[level, k, 1:3, 0], ZA.at[level, k], za_s.at[level, k], za_r.at[level, k], {"az": down}
        )

    def z_i(level, k):
        return remote(
            I.at[level, k, 1:3, planes - 1], ZI.at[level, k], zi_s.at[level, k], zi_r.at[level, k], {"az": up}
        )

    def ax_a(level, k):
        return remote(SA.at[level, k], AA.at[level, k], aa_s.at[level, k], aa_r.at[level, k], {"ax": ax - 1})

    def ax_i(level, k):
        return remote(SI.at[level, k], AI.at[level, k], ai_s.at[level, k], ai_r.at[level, k], {"ax": ax + 1})

    def out_here(which, k):
        src, dst = ((X.at[2, k], sol), (RS.at[k], res))[which]
        return pltpu.make_async_copy(src.at[:, mine], dst.at[half * side + k], o_l.at[which, k])

    def out_away(which, k):
        src, dst = ((X.at[2, k], sol), (RS.at[k], res))[which]
        return remote(
            src.at[:, theirs], dst.at[half * side + k], o_s.at[which, k], o_r.at[which, k], {"az": partner}
        )

    def out_foreign(which, k):
        src, dst = ((XF.at[k], sol), (RF.at[k], res))[which]
        return pltpu.make_async_copy(src, dst.at[half * (1 - side) + k], f_l.at[which, k])

    def hand_x(k):
        return remote(X.at[2, k, :, theirs], XF.at[k], xf_s.at[k], xf_r.at[k], {"az": partner})

    def hand_a(k, src):
        return remote(src, HA.at[k], ha_s.at[k], ha_r.at[k], {"az": partner})

    def hand_i(k, src):
        return remote(src, HI.at[k], hi_s.at[k], hi_r.at[k], {"az": partner})

    def far_a(k):
        return remote(SFA.at[k], FA.at[k], fa_s.at[k], fa_r.at[k], {"ax": ax - 1})

    def far_i(k):
        return remote(SFI.at[k], FI.at[k], fi_s.at[k], fi_r.at[k], {"ax": ax + 1})

    operands = [
        pltpu.make_async_copy(src, dst, ops.at[j])
        for j, (src, dst) in enumerate(
            ((rel_in, rel), (lam_in, lam), (mag_in, mag), (reg_in, reg), (pcs_in, pcs), (smap_in, smap))
        )
    ]
    for copy in operands:
        copy.start()
    local_in().start()
    barrier = pltpu.get_barrier_semaphore()
    for step in range(1, n_az):
        pl.semaphore_signal(
            barrier, inc=1, device_id={"az": lax.rem(az + step, n_az)}, device_id_type=MESH
        )

    @pl.when(has_below)
    def _():
        pl.semaphore_signal(barrier, inc=1, device_id={"ax": ax - 1}, device_id_type=MESH)

    @pl.when(has_above)
    def _():
        pl.semaphore_signal(barrier, inc=1, device_id={"ax": ax + 1}, device_id_type=MESH)

    for copy in operands:
        copy.wait()
    for p in range(cells):
        G[0, cells * side + p] = rel[0, p]
        G[1, cells * side + p] = rel[1, p] * (1.0 + 3.0 * lam[p].astype(F32))
        G[2, cells * side + p] = rel[2, p]
        G[3, cells * side + p] = jnp.where(mag[p] == 1, reg[p] - az * slots, -1).astype(F32)
    PG[az] = pcs[...]

    pl.semaphore_wait(barrier, n_az - 1 + has_below.astype(jnp.int32) + has_above.astype(jnp.int32))

    swap_in(0).start()
    for step in range(1, n_az):
        give_pieces(step).start()
    swap_g().start()

    for k in range(1, AHEAD):
        swap_in(k).start()

    @pl.when(jnp.logical_not(has_above))
    def _():
        AA[...] = jnp.zeros_like(AA)
        FA[...] = jnp.zeros_like(FA)

    @pl.when(jnp.logical_not(has_below))
    def _():
        AI[...] = jnp.zeros_like(AI)
        FI[...] = jnp.zeros_like(FI)

    row_of = lax.broadcasted_iota(jnp.int32, (rows, radial), 0)
    lane_of = lax.broadcasted_iota(jnp.int32, (rows, radial), 1)

    def next_radial(v):
        return jnp.where(lane_of == radial - 1, 0.0, pltpu.roll(v, radial - 1, 1))

    def prev_radial(v):
        return jnp.where(lane_of == 0, 0.0, pltpu.roll(v, 1, 1))

    def next_axial(v, halo):
        return jnp.where(row_of == rows - 1, halo, pltpu.roll(v, rows - 1, 0))

    def prev_axial(v, halo):
        return jnp.where(row_of == 0, halo, pltpu.roll(v, 1, 0))

    def flux_of(a0, a1, a2, b1, b2, h0, h2):
        return (
            (next_axial(a2, h2) - a2) - (next_radial(a1) - a1),
            (next_radial(a0) - a0) - (b2 - a2),
            (b1 - a1) - (next_axial(a0, h0) - a0),
        )

    def curl_of(i0, i1, i2, b1, b2, h0, h2):
        return (
            (i2 - prev_axial(i2, h2)) - (i1 - prev_radial(i1)),
            (i0 - prev_radial(i0)) - (i2 - b2),
            (i1 - b1) - (i0 - prev_axial(i0, h0)),
        )

    def send_a(level, k):
        z_a(level, k).start()
        for p in range(planes):
            for j, c in enumerate((0, 2)):
                SA[level, k, j * planes + p : j * planes + p + 1, :] = X[level, k, c, p, 0:1, :]

        @pl.when(has_below)
        def _():
            ax_a(level, k).start()

    def sources(k):
        table = TAB[...]
        lane = lax.broadcasted_iota(jnp.int32, table.shape[1:], 1)
        for c in range(3):
            column = jnp.sum(jnp.where(lane == half * side + k, table[c], 0.0), axis=1, keepdims=True)
            values = [jnp.broadcast_to(column[j : j + 1], (rows, radial)) for j in range(2 * slots)]
            for p in range(planes):
                code = G[3, p]
                total = jnp.zeros((rows, radial), F32)
                for j in range(slots):
                    total = jnp.where(code == float(j), values[p // cells * slots + j], total)
                NS[k, c, p] = G[c, p] * total

    def intensity(level, k):
        z_a(level, k).wait_recv()

        @pl.when(has_above)
        def _():
            ax_a(level, k).wait_recv()

        for p in reversed(range(planes)):
            a0, a1, a2 = X[level, k, 0, p], X[level, k, 1, p], X[level, k, 2, p]
            if p < planes - 1:
                b1, b2 = X[level, k, 1, p + 1], X[level, k, 2, p + 1]
            else:
                b1, b2 = ZA[level, k, 0], ZA[level, k, 1]
            h0 = AA[level, k, p : p + 1, :]
            h2 = AA[level, k, planes + p : planes + p + 1, :]
            flux = flux_of(a0, a1, a2, b1, b2, h0, h2)
            for c, f in enumerate(flux):
                value = G[c, p] * f - NS[k, c, p]
                I[level, k, c, p] = value
                if c != 1:
                    at = (0 if c == 0 else planes) + p
                    SI[level, k, at : at + 1, :] = value[rows - 1 : rows, :]
            if p == planes - 1:
                z_i(level, k).start()

        @pl.when(has_above)
        def _():
            ax_i(level, k).start()

    def curl(level, k):
        z_i(level, k).wait_recv()

        @pl.when(has_below)
        def _():
            ax_i(level, k).wait_recv()

        for p in range(planes):
            i0, i1, i2 = I[level, k, 0, p], I[level, k, 1, p], I[level, k, 2, p]
            if p > 0:
                b1, b2 = I[level, k, 1, p - 1], I[level, k, 2, p - 1]
            else:
                b1, b2 = ZI[level, k, 0], ZI[level, k, 1]
            h0 = AI[level, k, p : p + 1, :]
            h2 = AI[level, k, planes + p : planes + p + 1, :]
            turned = curl_of(i0, i1, i2, b1, b2, h0, h2)
            for c, value in enumerate(turned):
                field = X[level, k, c, p]
                r = -value - mass_term * field
                if level == 2:
                    RS[k, c, p] = r
                elif level == 0:
                    d = r * (1.0 / cheb_centre)
                    D0[k, c, p] = d
                    X[1, k, c, p] = field + d
                else:
                    d = (rho_second * rho_first) * D0[k, c, p] + (2.0 * rho_second / cheb_halfwidth) * r
                    X[2, k, c, p] = field + d
        if level == 2:
            out_away(1, k).start()
            out_here(1, k).start()
        else:
            send_a(level + 1, k)
        if level == 1:
            @pl.when(k < short)
            def _():
                hand_x(k).start()

            @pl.when(k >= short)
            def _():
                out_away(0, k).start()

            out_here(0, k).start()

    def hand_ahead(k):
        @pl.when(side == 0)
        def _():
            hand_a(k, ZA.at[2, k]).start()
            hand_i(k, I.at[2, k, 1:3, cells - 1]).start()

        @pl.when(side == 1)
        def _():
            hand_a(k, X.at[2, k, 1:3, cells]).start()

    def last_curl(k):
        z_i(2, k).wait_recv()

        @pl.when(side == 1)
        def _():
            hand_i(k, ZI.at[2, k]).start()

        @pl.when(has_below)
        def _():
            ax_i(2, k).wait_recv()

        for q in range(cells):
            p = cells * side + q
            i0, i1, i2 = I[2, k, 0, p], I[2, k, 1, p], I[2, k, 2, p]
            if q > 0:
                b1, b2 = I[2, k, 1, p - 1], I[2, k, 2, p - 1]
            else:
                b1 = jnp.where(side == 0, ZI[2, k, 0], I[2, k, 1, cells - 1])
                b2 = jnp.where(side == 0, ZI[2, k, 1], I[2, k, 2, cells - 1])
            h0, h2 = (
                jnp.where(side == 0, AI[2, k, at : at + 1, :], AI[2, k, at + cells : at + cells + 1, :])
                for at in (q, planes + q)
            )
            for c, value in enumerate(curl_of(i0, i1, i2, b1, b2, h0, h2)):
                RS[k, c, p] = -value - mass_term * X[2, k, c, p]
        out_here(1, k).start()

    def far_start(k):
        hand_x(k).wait_recv()
        out_foreign(0, k).start()
        for q in range(cells):
            for j, c in enumerate((0, 2)):
                SFA[k, j * cells + q : j * cells + q + 1, :] = XF[k, c, q, 0:1, :]

        @pl.when(has_below)
        def _():
            far_a(k).start()

    def far_intensity(k):
        hand_a(k, ZA.at[2, k]).wait_recv()

        @pl.when(has_above)
        def _():
            far_a(k).wait_recv()

        table = TAB[...]
        lane = lax.broadcasted_iota(jnp.int32, table.shape[1:], 1)
        for q in range(cells):
            p = cells * side + q
            a0, a1, a2 = XF[k, 0, q], XF[k, 1, q], XF[k, 2, q]
            if q < cells - 1:
                b1, b2 = XF[k, 1, q + 1], XF[k, 2, q + 1]
            else:
                b1, b2 = HA[k, 0], HA[k, 1]
            h0, h2 = FA[k, q : q + 1, :], FA[k, cells + q : cells + q + 1, :]
            code = G[3, p]
            for c, f in enumerate(flux_of(a0, a1, a2, b1, b2, h0, h2)):
                column = jnp.sum(
                    jnp.where(lane == half * (1 - side) + k, table[c], 0.0), axis=1, keepdims=True
                )
                total = jnp.zeros((rows, radial), F32)
                for j in range(slots):
                    own = jnp.where(side == 0, column[j : j + 1], column[slots + j : slots + j + 1])
                    total = jnp.where(code == float(j), jnp.broadcast_to(own, (rows, radial)), total)
                value = G[c, p] * (f - total)
                IF[k, c, q] = value
                if c != 1:
                    at = (0 if c == 0 else cells) + q
                    SFI[k, at : at + 1, :] = value[rows - 1 : rows, :]

        @pl.when(has_above)
        def _():
            far_i(k).start()

    def far_curl(k):
        hand_i(k, ZI.at[2, k]).wait_recv()

        @pl.when(has_below)
        def _():
            far_i(k).wait_recv()

        for q in range(cells):
            i0, i1, i2 = IF[k, 0, q], IF[k, 1, q], IF[k, 2, q]
            if q > 0:
                b1, b2 = IF[k, 1, q - 1], IF[k, 2, q - 1]
            else:
                b1, b2 = HI[k, 0], HI[k, 1]
            h0, h2 = FI[k, q : q + 1, :], FI[k, cells + q : cells + q + 1, :]
            for c, value in enumerate(curl_of(i0, i1, i2, b1, b2, h0, h2)):
                RF[k, c, q] = -value - mass_term * XF[k, c, q]
        out_foreign(1, k).start()

    def stage(s, k):
        if s == 0:
            @pl.when(k == 0)
            def _():
                local_in().wait()

            swap_in(k).wait_recv()

            @pl.when(k + AHEAD < half)
            def _():
                swap_in(k + AHEAD).start()

            send_a(0, k)
        elif s == 1:
            @pl.when(k == 0)
            def _():
                for step in range(1, n_az):
                    give_pieces(step).wait_recv()
                turned_map[...] = jnp.zeros_like(turned_map)
                turned_map[0:devs, 0 : smap.shape[1]] = smap[...].astype(F32)
                turned_map[...] = jnp.transpose(turned_map[...])
                base = pl.multiple_of((az - side) * slots, 2 * slots)
                own = turned_map[pl.ds(base, 2 * slots), 0:devs]

                for c in range(3):
                    def add(p, total, c=c):
                        for q in range(slots):
                            total = total + jnp.where(own == (p * slots + q).astype(F32), PG[p, c, q : q + 1, :], 0.0)
                        return total

                    TAB[c] = lax.fori_loop(0, n_az, add, jnp.zeros(own.shape, F32))
                swap_g().wait_recv()

            sources(k)
            intensity(0, k)
        elif s == 5:
            intensity(2, k)

            @pl.when(k < short)
            def _():
                hand_ahead(k)
        elif s == 6:
            @pl.when(k < short)
            def _():
                last_curl(k)

            @pl.when(k >= short)
            def _():
                curl(2, k)
        elif s % 2 == 0:
            curl(s // 2 - 1, k)
        else:
            intensity(s // 2, k)

    def grouped(work, chunk, count):
        @pl.when(jnp.logical_and(chunk >= 0, chunk < count // GROUP))
        def _():
            def one(d, inner):
                work(chunk * GROUP + d)
                return inner

            lax.fori_loop(0, GROUP, one, 0)

    def wave(t, carry):
        for s in reversed(range(1 + 2 * LEVELS)):
            grouped(functools.partial(stage, s), t - s, half)
        for s, work in ((8, far_curl), (7, far_intensity), (6, far_start)):
            grouped(work, t - s, short)
        return carry

    lax.fori_loop(0, max(half // GROUP + 6, short // GROUP + 8), wave, 0)

    for step in range(1, n_az):
        give_pieces(step).wait_send()
    swap_g().wait_send()

    def finish(k, carry):
        swap_in(k).wait_send()
        for level in range(LEVELS):
            z_a(level, k).wait_send()
            z_i(level, k).wait_send()

            @pl.when(has_below)
            def _():
                ax_a(level, k).wait_send()

            @pl.when(has_above)
            def _():
                ax_i(level, k).wait_send()

        for which in range(2):
            out_here(which, k).wait()
        return carry

    lax.fori_loop(0, half, finish, 0)

    def finish_short(k, carry):
        hand_x(k).wait_send()
        hand_a(k, ZA.at[2, k]).wait_send()
        hand_i(k, ZI.at[2, k]).wait_send()

        @pl.when(has_below)
        def _():
            far_a(k).wait_send()

        @pl.when(has_above)
        def _():
            far_i(k).wait_send()

        for which in range(2):
            out_foreign(which, k).wait()
        return carry

    lax.fori_loop(0, short, finish_short, 0)

    def finish_plain(k, carry):
        for which in range(2):
            out_away(which, k).wait()
        return carry

    lax.fori_loop(short, half, finish_plain, 0)


def hand_over(a, b, a_out, b_out, held, in_sems, out_sems):
    parts = in_sems.shape[1]
    share = a.shape[0] // parts

    def pair(i, j):
        src, dst = ((a, a_out), (b, b_out))[i]
        rows = pl.ds(j * share, share)
        return (
            pltpu.make_async_copy(src.at[rows], held.at[i, rows], in_sems.at[i, j]),
            pltpu.make_async_copy(held.at[i, rows], dst.at[rows], out_sems.at[i, j]),
        )

    pairs = [pair(i, j) for j in range(parts) for i in range(2)]
    for first, _ in pairs:
        first.start()
    for first, second in pairs:
        first.wait()
        second.start()
    for _, second in pairs:
        second.wait()


def shards(n_az, n_ax, start_field, reluctivity, lamination, magnets, region_ids, pieces, slot_map):
    devs, comps, cells, rows, radial = start_field.shape
    slots = pieces.shape[2]
    half, planes = devs // 2, 2 * cells
    by_slot = jnp.transpose(pieces, (0, 2, 1))
    regions = slot_map.shape[1]
    square = -(-max(regions, devs) // 128) * 128

    tile = (rows, radial)
    dma = pltpu.SemaphoreType.DMA
    phase = (LEVELS, half)
    anywhere = pl.BlockSpec(memory_space=pl.ANY)
    block = (half, comps, planes) + tile
    home = (half, comps, cells) + tile
    shape = jax.ShapeDtypeStruct(start_field.shape, F32)
    field, left = pl.pallas_call(
        functools.partial(kernel, n_az, n_ax, devs, cells, slots),
        out_shape=(shape, shape),
        in_specs=[anywhere] * 7,
        out_specs=(anywhere, anywhere),
        scratch_shapes=[
            pltpu.VMEM(reluctivity.shape, F32),
            pltpu.VMEM(lamination.shape, jnp.int32),
            pltpu.VMEM(lamination.shape, jnp.int32),
            pltpu.VMEM(lamination.shape, jnp.int32),
            pltpu.VMEM(by_slot.shape, F32),
            pltpu.VMEM(slot_map.shape, jnp.int32),
            pltpu.VMEM((square, square), F32),
            pltpu.VMEM((LEVELS,) + block, F32),
            pltpu.VMEM(block, F32),
            pltpu.VMEM((LEVELS,) + block, F32),
            pltpu.VMEM(block, F32),
            pltpu.VMEM(block, F32),
            pltpu.VMEM((comps + 1, planes) + tile, F32),
            pltpu.VMEM((n_az,) + by_slot.shape, F32),
            pltpu.VMEM((comps, 2 * slots, devs), F32),
            pltpu.VMEM(phase + (2,) + tile, F32),
            pltpu.VMEM(phase + (2,) + tile, F32),
        ]
        + [pltpu.VMEM(phase + (2 * planes, radial), F32)] * 4
        + [pltpu.VMEM(home, F32)] * 3
        + [pltpu.VMEM((half, 2) + tile, F32)] * 2
        + [pltpu.VMEM((half, 2 * cells, radial), F32)] * 4
        + [dma((6,)), dma, dma((half,)), dma((half,)), dma, dma, dma((n_az,)), dma((n_az,))]
        + [dma(phase)] * 8
        + [dma((2, half))] * 4
        + [dma((half,))] * 10,
        compiler_params=pltpu.CompilerParams(
            collective_id=0, has_side_effects=True, vmem_limit_bytes=60 * 1024 * 1024
        ),
        cost_estimate=pl.CostEstimate(
            flops=150 * start_field.size, bytes_accessed=12 * start_field.size, transcendentals=0
        ),
    )(start_field, reluctivity, lamination, magnets, region_ids, by_slot, slot_map)
    return pl.pallas_call(
        hand_over,
        out_shape=(shape, shape),
        in_specs=[anywhere] * 2,
        out_specs=(anywhere, anywhere),
        scratch_shapes=[pltpu.VMEM((2,) + start_field.shape, F32), dma((2, 4)), dma((2, 4))],
        compiler_params=pltpu.CompilerParams(vmem_limit_bytes=60 * 1024 * 1024),
        cost_estimate=pl.CostEstimate(flops=0, bytes_accessed=16 * start_field.size, transcendentals=0),
    )(field, left)


def solution(mesh):
    placed = (
        P(None, None, "az", "ax", None),
        P(None, "az", "ax", None),
        P("az", "ax", None),
        P("az", "ax", None),
        P("az", "ax", None),
        P(None, None, "az"),
        P(),
    )
    return jax.shard_map(
        functools.partial(shards, mesh.shape["az"], mesh.shape["ax"]),
        mesh=mesh,
        in_specs=placed,
        out_specs=(P(None, None, "az", "ax", None), P(None, None, "az", "ax", None)),
        check_vma=False,
    )
```

```python
import functools

import jax
import jax.numpy as jnp
from jax import lax
from jax.experimental import pallas as pl
from jax.experimental.pallas import tpu as pltpu
from jax.sharding import PartitionSpec as P

mass_term = 1.0
cheb_centre = 8.5
cheb_halfwidth = 7.5
cheb_sigma = cheb_centre / cheb_halfwidth
rho_first = 1.0 / cheb_sigma
rho_second = 1.0 / (2.0 * cheb_sigma - rho_first)

MESH = pl.DeviceIdType.MESH
F32 = jnp.float32
LEVELS = 3
GROUP = 2
AHEAD = 3
PLAIN = 2


def kernel(
    n_az, n_ax, devs, cells, slots,
    start, rel_in, lam_in, mag_in, reg_in, pcs_in, smap_in,
    sol, res,
    rel, lam, mag, reg, pcs, smap, turned_map,
    X, D0, I, NS, RS, G, PG, TAB, ZA, ZI, AA, AI, SA, SI,
    XF, IF, RF, HA, HI, FA, FI, SFA, SFI,
    ops, in_loc, in_s, in_r, g_s, g_r, p_s, p_r,
    za_s, za_r, zi_s, zi_r, aa_s, aa_r, ai_s, ai_r, o_l, f_l, o_s, o_r,
    xf_s, xf_r, ha_s, ha_r, hi_s, hi_r, fa_s, fa_r, fi_s, fi_r,
):
    half = devs // 2
    short = half - PLAIN
    planes = 2 * cells
    rows, radial = X.shape[-2], X.shape[-1]
    az, ax = lax.axis_index("az"), lax.axis_index("ax")
    side = lax.rem(az, 2)
    partner = az + 1 - 2 * side
    up, down = lax.rem(az + 2, n_az), lax.rem(az + n_az - 2, n_az)
    mine = pl.ds(cells * side, cells)
    theirs = pl.ds(cells * (1 - side), cells)
    has_below, has_above = ax > 0, ax < n_ax - 1

    def remote(src, dst, s, r, where):
        return pltpu.make_async_remote_copy(
            src_ref=src, dst_ref=dst, send_sem=s, recv_sem=r, device_id=where, device_id_type=MESH
        )

    def local_in():
        return pltpu.make_async_copy(start.at[pl.ds(half * side, half)], X.at[0, :, :, mine], in_loc)

    def swap_in(k):
        return remote(
            start.at[half * (1 - side) + k], X.at[0, k, :, mine], in_s.at[k], in_r.at[k], {"az": partner}
        )

    def swap_g():
        return remote(G.at[:, mine], G.at[:, mine], g_s, g_r, {"az": partner})

    def give_pieces(step):
        return remote(PG.at[az], PG.at[az], p_s.at[step], p_r.at[step], {"az": lax.rem(az + step, n_az)})

    def z_a(level, k):
        return remote(
            X.at[level, k, 1:3, 0], ZA.at[level, k], za_s.at[level, k], za_r.at[level, k], {"az": down}
        )

    def z_i(level, k):
        return remote(
            I.at[level, k, 1:3, planes - 1], ZI.at[level, k], zi_s.at[level, k], zi_r.at[level, k], {"az": up}
        )

    def ax_a(level, k):
        return remote(SA.at[level, k], AA.at[level, k], aa_s.at[level, k], aa_r.at[level, k], {"ax": ax - 1})

    def ax_i(level, k):
        return remote(SI.at[level, k], AI.at[level, k], ai_s.at[level, k], ai_r.at[level, k], {"ax": ax + 1})

    def out_here(which, k):
        src, dst = ((X.at[2, k], sol), (RS.at[k], res))[which]
        return pltpu.make_async_copy(src.at[:, mine], dst.at[half * side + k], o_l.at[which, k])

    def out_away(which, k):
        src, dst = ((X.at[2, k], sol), (RS.at[k], res))[which]
        return remote(
            src.at[:, theirs], dst.at[half * side + k], o_s.at[which, k], o_r.at[which, k], {"az": partner}
        )

    def out_foreign(which, k):
        src, dst = ((XF.at[k], sol), (RF.at[k], res))[which]
        return pltpu.make_async_copy(src, dst.at[half * (1 - side) + k], f_l.at[which, k])

    def hand_x(k):
        return remote(X.at[2, k, :, theirs], XF.at[k], xf_s.at[k], xf_r.at[k], {"az": partner})

    def hand_a(k, src):
        return remote(src, HA.at[k], ha_s.at[k], ha_r.at[k], {"az": partner})

    def hand_i(k, src):
        return remote(src, HI.at[k], hi_s.at[k], hi_r.at[k], {"az": partner})

    def far_a(k):
        return remote(SFA.at[k], FA.at[k], fa_s.at[k], fa_r.at[k], {"ax": ax - 1})

    def far_i(k):
        return remote(SFI.at[k], FI.at[k], fi_s.at[k], fi_r.at[k], {"ax": ax + 1})

    operands = [
        pltpu.make_async_copy(src, dst, ops.at[j])
        for j, (src, dst) in enumerate(
            ((rel_in, rel), (lam_in, lam), (mag_in, mag), (reg_in, reg), (pcs_in, pcs), (smap_in, smap))
        )
    ]
    for copy in operands:
        copy.start()
    local_in().start()
    barrier = pltpu.get_barrier_semaphore()
    for step in range(1, n_az):
        pl.semaphore_signal(
            barrier, inc=1, device_id={"az": lax.rem(az + step, n_az)}, device_id_type=MESH
        )

    @pl.when(has_below)
    def _():
        pl.semaphore_signal(barrier, inc=1, device_id={"ax": ax - 1}, device_id_type=MESH)

    @pl.when(has_above)
    def _():
        pl.semaphore_signal(barrier, inc=1, device_id={"ax": ax + 1}, device_id_type=MESH)

    for copy in operands:
        copy.wait()
    for p in range(cells):
        G[0, cells * side + p] = rel[0, p]
        G[1, cells * side + p] = rel[1, p] * (1.0 + 3.0 * lam[p].astype(F32))
        G[2, cells * side + p] = rel[2, p]
        G[3, cells * side + p] = jnp.where(mag[p] == 1, reg[p] - az * slots, -1).astype(F32)
    PG[az] = pcs[...]

    pl.semaphore_wait(barrier, n_az - 1 + has_below.astype(jnp.int32) + has_above.astype(jnp.int32))

    swap_in(0).start()
    for step in range(1, n_az):
        give_pieces(step).start()
    swap_g().start()

    for k in range(1, AHEAD):
        swap_in(k).start()

    @pl.when(jnp.logical_not(has_above))
    def _():
        AA[...] = jnp.zeros_like(AA)
        FA[...] = jnp.zeros_like(FA)

    @pl.when(jnp.logical_not(has_below))
    def _():
        AI[...] = jnp.zeros_like(AI)
        FI[...] = jnp.zeros_like(FI)

    row_of = lax.broadcasted_iota(jnp.int32, (rows, radial), 0)
    lane_of = lax.broadcasted_iota(jnp.int32, (rows, radial), 1)

    def next_radial(v):
        return jnp.where(lane_of == radial - 1, 0.0, pltpu.roll(v, radial - 1, 1))

    def prev_radial(v):
        return jnp.where(lane_of == 0, 0.0, pltpu.roll(v, 1, 1))

    def next_axial(v, halo):
        return jnp.where(row_of == rows - 1, halo, pltpu.roll(v, rows - 1, 0))

    def prev_axial(v, halo):
        return jnp.where(row_of == 0, halo, pltpu.roll(v, 1, 0))

    def flux_of(a0, a1, a2, b1, b2, h0, h2):
        return (
            (next_axial(a2, h2) - a2) - (next_radial(a1) - a1),
            (next_radial(a0) - a0) - (b2 - a2),
            (b1 - a1) - (next_axial(a0, h0) - a0),
        )

    def curl_of(i0, i1, i2, b1, b2, h0, h2):
        return (
            (i2 - prev_axial(i2, h2)) - (i1 - prev_radial(i1)),
            (i0 - prev_radial(i0)) - (i2 - b2),
            (i1 - b1) - (i0 - prev_axial(i0, h0)),
        )

    def send_a(level, k):
        z_a(level, k).start()
        for p in range(planes):
            for j, c in enumerate((0, 2)):
                SA[level, k, j * planes + p : j * planes + p + 1, :] = X[level, k, c, p, 0:1, :]

        @pl.when(has_below)
        def _():
            ax_a(level, k).start()

    def sources(k):
        table = TAB[...]
        lane = lax.broadcasted_iota(jnp.int32, table.shape[1:], 1)
        for c in range(3):
            column = jnp.sum(jnp.where(lane == half * side + k, table[c], 0.0), axis=1, keepdims=True)
            values = [jnp.broadcast_to(column[j : j + 1], (rows, radial)) for j in range(2 * slots)]
            for p in range(planes):
                code = G[3, p]
                total = jnp.zeros((rows, radial), F32)
                for j in range(slots):
                    total = jnp.where(code == float(j), values[p // cells * slots + j], total)
                NS[k, c, p] = G[c, p] * total

    def intensity(level, k):
        z_a(level, k).wait_recv()

        @pl.when(has_above)
        def _():
            ax_a(level, k).wait_recv()

        for p in reversed(range(planes)):
            a0, a1, a2 = X[level, k, 0, p], X[level, k, 1, p], X[level, k, 2, p]
            if p < planes - 1:
                b1, b2 = X[level, k, 1, p + 1], X[level, k, 2, p + 1]
            else:
                b1, b2 = ZA[level, k, 0], ZA[level, k, 1]
            h0 = AA[level, k, p : p + 1, :]
            h2 = AA[level, k, planes + p : planes + p + 1, :]
            flux = flux_of(a0, a1, a2, b1, b2, h0, h2)
            for c, f in enumerate(flux):
                value = G[c, p] * f - NS[k, c, p]
                I[level, k, c, p] = value
                if c != 1:
                    at = (0 if c == 0 else planes) + p
                    SI[level, k, at : at + 1, :] = value[rows - 1 : rows, :]
            if p == planes - 1:
                z_i(level, k).start()

        @pl.when(has_above)
        def _():
            ax_i(level, k).start()

    def curl(level, k):
        z_i(level, k).wait_recv()

        @pl.when(has_below)
        def _():
            ax_i(level, k).wait_recv()

        for p in range(planes):
            i0, i1, i2 = I[level, k, 0, p], I[level, k, 1, p], I[level, k, 2, p]
            if p > 0:
                b1, b2 = I[level, k, 1, p - 1], I[level, k, 2, p - 1]
            else:
                b1, b2 = ZI[level, k, 0], ZI[level, k, 1]
            h0 = AI[level, k, p : p + 1, :]
            h2 = AI[level, k, planes + p : planes + p + 1, :]
            turned = curl_of(i0, i1, i2, b1, b2, h0, h2)
            for c, value in enumerate(turned):
                field = X[level, k, c, p]
                r = -value - mass_term * field
                if level == 2:
                    RS[k, c, p] = r
                elif level == 0:
                    d = r * (1.0 / cheb_centre)
                    D0[k, c, p] = d
                    X[1, k, c, p] = field + d
                else:
                    d = (rho_second * rho_first) * D0[k, c, p] + (2.0 * rho_second / cheb_halfwidth) * r
                    X[2, k, c, p] = field + d
        if level == 2:
            out_away(1, k).start()
            out_here(1, k).start()
        else:
            send_a(level + 1, k)
        if level == 1:
            @pl.when(k < short)
            def _():
                hand_x(k).start()

            @pl.when(k >= short)
            def _():
                out_away(0, k).start()

            out_here(0, k).start()

    def hand_ahead(k):
        @pl.when(side == 0)
        def _():
            hand_a(k, ZA.at[2, k]).start()
            hand_i(k, I.at[2, k, 1:3, cells - 1]).start()

        @pl.when(side == 1)
        def _():
            hand_a(k, X.at[2, k, 1:3, cells]).start()

    def last_curl(k):
        z_i(2, k).wait_recv()

        @pl.when(side == 1)
        def _():
            hand_i(k, ZI.at[2, k]).start()

        @pl.when(has_below)
        def _():
            ax_i(2, k).wait_recv()

        for q in range(cells):
            p = cells * side + q
            i0, i1, i2 = I[2, k, 0, p], I[2, k, 1, p], I[2, k, 2, p]
            if q > 0:
                b1, b2 = I[2, k, 1, p - 1], I[2, k, 2, p - 1]
            else:
                b1 = jnp.where(side == 0, ZI[2, k, 0], I[2, k, 1, cells - 1])
                b2 = jnp.where(side == 0, ZI[2, k, 1], I[2, k, 2, cells - 1])
            h0, h2 = (
                jnp.where(side == 0, AI[2, k, at : at + 1, :], AI[2, k, at + cells : at + cells + 1, :])
                for at in (q, planes + q)
            )
            for c, value in enumerate(curl_of(i0, i1, i2, b1, b2, h0, h2)):
                RS[k, c, p] = -value - mass_term * X[2, k, c, p]
        out_here(1, k).start()

    def far_start(k):
        hand_x(k).wait_recv()
        out_foreign(0, k).start()
        for q in range(cells):
            for j, c in enumerate((0, 2)):
                SFA[k, j * cells + q : j * cells + q + 1, :] = XF[k, c, q, 0:1, :]

        @pl.when(has_below)
        def _():
            far_a(k).start()

    def far_intensity(k):
        hand_a(k, ZA.at[2, k]).wait_recv()

        @pl.when(has_above)
        def _():
            far_a(k).wait_recv()

        table = TAB[...]
        lane = lax.broadcasted_iota(jnp.int32, table.shape[1:], 1)
        for q in range(cells):
            p = cells * side + q
            a0, a1, a2 = XF[k, 0, q], XF[k, 1, q], XF[k, 2, q]
            if q < cells - 1:
                b1, b2 = XF[k, 1, q + 1], XF[k, 2, q + 1]
            else:
                b1, b2 = HA[k, 0], HA[k, 1]
            h0, h2 = FA[k, q : q + 1, :], FA[k, cells + q : cells + q + 1, :]
            code = G[3, p]
            for c, f in enumerate(flux_of(a0, a1, a2, b1, b2, h0, h2)):
                column = jnp.sum(
                    jnp.where(lane == half * (1 - side) + k, table[c], 0.0), axis=1, keepdims=True
                )
                total = jnp.zeros((rows, radial), F32)
                for j in range(slots):
                    own = jnp.where(side == 0, column[j : j + 1], column[slots + j : slots + j + 1])
                    total = jnp.where(code == float(j), jnp.broadcast_to(own, (rows, radial)), total)
                value = G[c, p] * (f - total)
                IF[k, c, q] = value
                if c != 1:
                    at = (0 if c == 0 else cells) + q
                    SFI[k, at : at + 1, :] = value[rows - 1 : rows, :]

        @pl.when(has_above)
        def _():
            far_i(k).start()

    def far_curl(k):
        hand_i(k, ZI.at[2, k]).wait_recv()

        @pl.when(has_below)
        def _():
            far_i(k).wait_recv()

        for q in range(cells):
            i0, i1, i2 = IF[k, 0, q], IF[k, 1, q], IF[k, 2, q]
            if q > 0:
                b1, b2 = IF[k, 1, q - 1], IF[k, 2, q - 1]
            else:
                b1, b2 = HI[k, 0], HI[k, 1]
            h0, h2 = FI[k, q : q + 1, :], FI[k, cells + q : cells + q + 1, :]
            for c, value in enumerate(curl_of(i0, i1, i2, b1, b2, h0, h2)):
                RF[k, c, q] = -value - mass_term * XF[k, c, q]
        out_foreign(1, k).start()

    def stage(s, k):
        if s == 0:
            @pl.when(k == 0)
            def _():
                local_in().wait()

            swap_in(k).wait_recv()

            @pl.when(k + AHEAD < half)
            def _():
                swap_in(k + AHEAD).start()

            send_a(0, k)
        elif s == 1:
            @pl.when(k == 0)
            def _():
                for step in range(1, n_az):
                    give_pieces(step).wait_recv()
                turned_map[...] = jnp.zeros_like(turned_map)
                turned_map[0:devs, 0 : smap.shape[1]] = smap[...].astype(F32)
                turned_map[...] = jnp.transpose(turned_map[...])
                base = pl.multiple_of((az - side) * slots, 2 * slots)
                own = turned_map[pl.ds(base, 2 * slots), 0:devs]

                for c in range(3):
                    def add(p, total, c=c):
                        for q in range(slots):
                            total = total + jnp.where(own == (p * slots + q).astype(F32), PG[p, c, q : q + 1, :], 0.0)
                        return total

                    TAB[c] = lax.fori_loop(0, n_az, add, jnp.zeros(own.shape, F32))
                swap_g().wait_recv()

            sources(k)
            intensity(0, k)
        elif s == 5:
            intensity(2, k)

            @pl.when(k < short)
            def _():
                hand_ahead(k)
        elif s == 6:
            @pl.when(k < short)
            def _():
                last_curl(k)

            @pl.when(k >= short)
            def _():
                curl(2, k)
        elif s % 2 == 0:
            curl(s // 2 - 1, k)
        else:
            intensity(s // 2, k)

    def grouped(work, chunk, count):
        @pl.when(jnp.logical_and(chunk >= 0, chunk < count // GROUP))
        def _():
            def one(d, inner):
                work(chunk * GROUP + d)
                return inner

            lax.fori_loop(0, GROUP, one, 0)

    def wave(t, carry):
        for s in reversed(range(1 + 2 * LEVELS)):
            grouped(functools.partial(stage, s), t - s, half)
        for s, work in ((7, far_curl), (6, far_intensity), (5, far_start)):
            grouped(work, t - s, short)
        return carry

    lax.fori_loop(0, max(half // GROUP + 6, short // GROUP + 7), wave, 0)

    for step in range(1, n_az):
        give_pieces(step).wait_send()
    swap_g().wait_send()

    def finish(k, carry):
        swap_in(k).wait_send()
        for level in range(LEVELS):
            z_a(level, k).wait_send()
            z_i(level, k).wait_send()

            @pl.when(has_below)
            def _():
                ax_a(level, k).wait_send()

            @pl.when(has_above)
            def _():
                ax_i(level, k).wait_send()

        for which in range(2):
            out_here(which, k).wait()
        return carry

    lax.fori_loop(0, half, finish, 0)

    def finish_short(k, carry):
        hand_x(k).wait_send()
        hand_a(k, ZA.at[2, k]).wait_send()
        hand_i(k, ZI.at[2, k]).wait_send()

        @pl.when(has_below)
        def _():
            far_a(k).wait_send()

        @pl.when(has_above)
        def _():
            far_i(k).wait_send()

        for which in range(2):
            out_foreign(which, k).wait()
        return carry

    lax.fori_loop(0, short, finish_short, 0)

    def finish_plain(k, carry):
        for which in range(2):
            out_away(which, k).wait()
        return carry

    lax.fori_loop(short, half, finish_plain, 0)


def hand_over(a, b, a_out, b_out, held, in_sems, out_sems):
    parts = in_sems.shape[1]
    share = a.shape[0] // parts

    def pair(i, j):
        src, dst = ((a, a_out), (b, b_out))[i]
        rows = pl.ds(j * share, share)
        return (
            pltpu.make_async_copy(src.at[rows], held.at[i, rows], in_sems.at[i, j]),
            pltpu.make_async_copy(held.at[i, rows], dst.at[rows], out_sems.at[i, j]),
        )

    pairs = [pair(i, j) for j in range(parts) for i in range(2)]
    for first, _ in pairs:
        first.start()
    for first, second in pairs:
        first.wait()
        second.start()
    for _, second in pairs:
        second.wait()


def shards(n_az, n_ax, start_field, reluctivity, lamination, magnets, region_ids, pieces, slot_map):
    devs, comps, cells, rows, radial = start_field.shape
    slots = pieces.shape[2]
    half, planes = devs // 2, 2 * cells
    by_slot = jnp.transpose(pieces, (0, 2, 1))
    regions = slot_map.shape[1]
    square = -(-max(regions, devs) // 128) * 128

    tile = (rows, radial)
    dma = pltpu.SemaphoreType.DMA
    phase = (LEVELS, half)
    anywhere = pl.BlockSpec(memory_space=pl.ANY)
    block = (half, comps, planes) + tile
    home = (half, comps, cells) + tile
    shape = jax.ShapeDtypeStruct(start_field.shape, F32)
    field, left = pl.pallas_call(
        functools.partial(kernel, n_az, n_ax, devs, cells, slots),
        out_shape=(shape, shape),
        in_specs=[anywhere] * 7,
        out_specs=(anywhere, anywhere),
        scratch_shapes=[
            pltpu.VMEM(reluctivity.shape, F32),
            pltpu.VMEM(lamination.shape, jnp.int32),
            pltpu.VMEM(lamination.shape, jnp.int32),
            pltpu.VMEM(lamination.shape, jnp.int32),
            pltpu.VMEM(by_slot.shape, F32),
            pltpu.VMEM(slot_map.shape, jnp.int32),
            pltpu.VMEM((square, square), F32),
            pltpu.VMEM((LEVELS,) + block, F32),
            pltpu.VMEM(block, F32),
            pltpu.VMEM((LEVELS,) + block, F32),
            pltpu.VMEM(block, F32),
            pltpu.VMEM(block, F32),
            pltpu.VMEM((comps + 1, planes) + tile, F32),
            pltpu.VMEM((n_az,) + by_slot.shape, F32),
            pltpu.VMEM((comps, 2 * slots, devs), F32),
            pltpu.VMEM(phase + (2,) + tile, F32),
            pltpu.VMEM(phase + (2,) + tile, F32),
        ]
        + [pltpu.VMEM(phase + (2 * planes, radial), F32)] * 4
        + [pltpu.VMEM(home, F32)] * 3
        + [pltpu.VMEM((half, 2) + tile, F32)] * 2
        + [pltpu.VMEM((half, 2 * cells, radial), F32)] * 4
        + [dma((6,)), dma, dma((half,)), dma((half,)), dma, dma, dma((n_az,)), dma((n_az,))]
        + [dma(phase)] * 8
        + [dma((2, half))] * 4
        + [dma((half,))] * 10,
        compiler_params=pltpu.CompilerParams(
            collective_id=0, has_side_effects=True, vmem_limit_bytes=60 * 1024 * 1024
        ),
        cost_estimate=pl.CostEstimate(
            flops=150 * start_field.size, bytes_accessed=12 * start_field.size, transcendentals=0
        ),
    )(start_field, reluctivity, lamination, magnets, region_ids, by_slot, slot_map)
    return pl.pallas_call(
        hand_over,
        out_shape=(shape, shape),
        in_specs=[anywhere] * 2,
        out_specs=(anywhere, anywhere),
        scratch_shapes=[pltpu.VMEM((2,) + start_field.shape, F32), dma((2, 4)), dma((2, 4))],
        compiler_params=pltpu.CompilerParams(vmem_limit_bytes=60 * 1024 * 1024),
        cost_estimate=pl.CostEstimate(flops=0, bytes_accessed=16 * start_field.size, transcendentals=0),
    )(field, left)


def solution(mesh):
    placed = (
        P(None, None, "az", "ax", None),
        P(None, "az", "ax", None),
        P("az", "ax", None),
        P("az", "ax", None),
        P("az", "ax", None),
        P(None, None, "az"),
        P(),
    )
    return jax.shard_map(
        functools.partial(shards, mesh.shape["az"], mesh.shape["ax"]),
        mesh=mesh,
        in_specs=placed,
        out_specs=(P(None, None, "az", "ax", None), P(None, None, "az", "ax", None)),
        check_vma=False,
    )
```
